512 devices in a mesh: seq: 256 (over y, x_hi, z, core), head: 2 (over x_lo).
Axes of the slice: x: 4 (x_hi: 2, x_lo: 2; x = x_hi * 2 + x_lo), y: 4, z: 16, core: 2. Of those that a mesh axis runs over, the one named last changes fastest.
Arguments:
- query: bfloat16 [131072, 8, 128], P('seq', 'head'), may hold values from -190 to 190
- key: bfloat16 [131072, 8, 128], P('seq', 'head'), may hold values from -7 to 7
- value: bfloat16 [131072, 8, 128], P('seq', 'head'), may hold values from -6 to 6
- dout: bfloat16 [131072, 8, 128], P('seq', 'head'), may hold values from -6 to 6
Outputs:
- attended: bfloat16 [131072, 8, 128], P('seq', 'head')
- grad_query: bfloat16 [131072, 8, 128], P('seq', 'head')
- grad_key: bfloat16 [131072, 8, 128], P('seq', 'head')
- grad_value: bfloat16 [131072, 8, 128], P('seq', 'head')
The draws below stay inside these ranges and needn't reach their ends.
All inputs are finite; a program needn't handle non-finite values.
Results may differ from the reference program's by a relative error of at most 0.012.
The reference program's roundings to bfloat16 on the way count: a program that leaves them out, or rounds other values in their place, can miss the bound.
Values may be sent and summed in bfloat16 or wider, within the bound.
No kernel may reach another device: no remote copies, remote signals or barrier semaphores. Data moves between devices by JAX's collectives and lax.ppermute only.
A program may use at most 128 MiB of HBM per device.

```python
import math
import jax
import jax.numpy as jnp
from jax import lax

HEAD_DIM = 128
HEADS = 8
TOK_DEV = 512
BLOCK = 256
LEVELS = 3
TOKENS = 131072


def key_rows(key):
    base = jax.random.truncated_normal(key, -6.0, 6.0, (TOKENS, HEADS, HEAD_DIM), jnp.float32)
    return base


def draw_key(key, part):
    return key_rows(key).astype(jnp.bfloat16)


def draw_query(key, part):
    own = jax.random.fold_in(key, 7)
    rows = jax.random.truncated_normal(own, -6.0, 6.0, (TOKENS, HEADS, HEAD_DIM), jnp.float32)
    mixed = rows
    return jnp.clip(mixed, -190.0, 190.0).astype(jnp.bfloat16)


def level_of(stream_key, shape, shards, smallest, largest):
    level, own = 1.0, jax.random.fold_in(stream_key, 6)
    for axis_at, shards_of in shards:
        heights = jnp.exp(jax.random.uniform(jax.random.fold_in(own, axis_at), (shards_of,), jnp.float32, smallest / len(shards), largest / len(shards)))
        level = level * jnp.repeat(heights, shape[axis_at] // shards_of).reshape([-1 if axis == axis_at else 1 for axis in range(len(shape))])
    return level


def noise(stream_key, extent, spread, bound, shards=(), held_as=jnp.bfloat16):
    factor_of = level_of(stream_key, extent, shards, -0.22, 0.18) if shards else 1.0
    array = jax.random.normal(stream_key, extent, jnp.float32) * spread * factor_of
    return jnp.minimum(jnp.maximum(array, -bound), bound).astype(held_as)


def setup_inputs(seed: int = 0) -> dict:
    streams_of = jax.random.split(jax.random.key(seed), 5)
    query = draw_query(jax.random.fold_in(streams_of[4], 71), 0)
    key = draw_key(jax.random.fold_in(streams_of[4], 71), 0)
    value = noise(streams_of[2], (TOKENS, HEADS, HEAD_DIM), 1.0, 6.0, ((0, 256), (1, 2)))
    dout = noise(streams_of[3], (TOKENS, HEADS, HEAD_DIM), 1.0, 6.0, ((0, 256), (1, 2)))
    return dict(query=query, key=key, value=value, dout=dout)


def inner_product(form, left, right):
    return jnp.einsum(form, left.astype(jnp.float32), right.astype(jnp.float32))

def shift_spans(x, dist):
    level_count = x.shape[0]
    filler = jnp.zeros((abs(dist),) + x.shape[1:], x.dtype)
    if dist > 0:
        return jnp.concatenate([filler, x[:level_count - dist]], axis=0)
    return jnp.concatenate([x[-dist:], filler], axis=0)

def coarsen(x, factor):
    shape = x.shape
    grouped = x.astype(jnp.float32).reshape(shape[:-3] + (shape[-3] // factor, factor) + shape[-2:])
    return lax.optimization_barrier(jnp.mean(grouped, axis=-3)).astype(jnp.bfloat16)

def head_pass(query, dout, ext_key, ext_val, ext_ok, coarse_key, coarse_val, coarse_ok):
    window_span = query.shape[0]
    window_width = query.shape[1]
    softmax_scale = 1.0 / math.sqrt(window_width)
    level_count = (ext_key.shape[0] - window_span) // 2
    blocks = window_span // level_count
    query_block_rows = query.reshape(blocks, level_count, window_width)
    gradient_block_rows = dout.reshape(blocks, level_count, window_width)
    key_window = jnp.stack([ext_key[b * level_count:(b + 3) * level_count] for b in range(blocks)])
    value_window = jnp.stack([ext_val[b * level_count:(b + 3) * level_count] for b in range(blocks)])
    ok_win = jnp.stack([ext_ok[b * level_count:(b + 3) * level_count] for b in range(blocks)])
    fine_scores = inner_product('uzl,uhl->uzh', query_block_rows, key_window) * softmax_scale
    fine_scores = jnp.where(ok_win[:, None, :], fine_scores, -jnp.inf).reshape(window_span, 3 * level_count)
    parts = [fine_scores]
    means = []
    for level in range(len(coarse_key)):
        factor = 2 ** (level + 1)
        qmean = lax.optimization_barrier(jnp.mean(query.astype(jnp.float32).reshape(window_span // factor, factor, window_width), axis=1)).astype(jnp.bfloat16)
        coarse = inner_product('qe,ke->qk', qmean, coarse_key[level]) * softmax_scale + math.log(factor)
        coarse = jnp.where(coarse_ok[level][None, :], coarse, -jnp.inf)
        parts.append(jnp.repeat(coarse, factor, axis=0))
        means.append(qmean)
    scores = jnp.concatenate(parts, axis=1)
    top = lax.optimization_barrier(jnp.max(scores, axis=1, keepdims=True))
    lse = top + jnp.log(lax.optimization_barrier(jnp.sum(jnp.exp(scores - top), axis=1, keepdims=True)))
    prob = jnp.exp(scores - lse)
    rounded = prob.astype(jnp.bfloat16)
    fine_probability = rounded[:, :3 * level_count].reshape(blocks, level_count, 3 * level_count)
    attention_output = inner_product('vyg,vgl->vyl', fine_probability, value_window).reshape(window_span, window_width)
    probability_gradient = [inner_product('uzl,uhl->uzh', gradient_block_rows, value_window).reshape(window_span, 3 * level_count)]
    start = 3 * level_count
    for level in range(len(coarse_key)):
        size = coarse_key[level].shape[0]
        attention_output = attention_output + inner_product('qk,ke->qe', rounded[:, start:start + size], coarse_val[level])
        probability_gradient.append(inner_product('qe,ke->qk', dout, coarse_val[level]))
        start = start + size
    probability_gradient = jnp.concatenate(probability_gradient, axis=1)
    delta = lax.optimization_barrier(jnp.sum(prob * probability_gradient, axis=1, keepdims=True))
    dscore = (prob * (probability_gradient - delta)).astype(jnp.bfloat16)
    fine_score_gradient = dscore[:, :3 * level_count].reshape(blocks, level_count, 3 * level_count)
    query_gradient = inner_product('vyg,vgl->vyl', fine_score_gradient, key_window).reshape(window_span, window_width) * softmax_scale
    key_window_gradient = inner_product('lrt,lrv->ltv', fine_score_gradient, query_block_rows) * softmax_scale
    value_window_gradient = inner_product('lrt,lrv->ltv', fine_probability, gradient_block_rows)
    dext_k = jnp.zeros(ext_key.shape, jnp.float32)
    dext_v = jnp.zeros(ext_key.shape, jnp.float32)
    for b in range(blocks):
        dext_k = dext_k + jnp.pad(key_window_gradient[b], ((b * level_count, (blocks - 1 - b) * level_count), (0, 0)))
        dext_v = dext_v + jnp.pad(value_window_gradient[b], ((b * level_count, (blocks - 1 - b) * level_count), (0, 0)))
    grad_ck = []
    grad_cv = []
    start = 3 * level_count
    for level in range(len(coarse_key)):
        factor = 2 ** (level + 1)
        size = coarse_key[level].shape[0]
        piece_ds = dscore[:, start:start + size]
        piece_p = rounded[:, start:start + size]
        rows = inner_product('qk,ke->qe', piece_ds, coarse_key[level]) * softmax_scale
        group = lax.optimization_barrier(jnp.mean(rows.reshape(window_span // factor, factor, window_width), axis=1))
        query_gradient = query_gradient + jnp.repeat(group, factor, axis=0)
        qrep = jnp.repeat(means[level], factor, axis=0)
        grad_ck.append(inner_product('qk,qe->ke', piece_ds, qrep) * softmax_scale)
        grad_cv.append(inner_product('qk,qe->ke', piece_p, dout))
        start = start + size
    return (attention_output.astype(jnp.bfloat16), query_gradient, dext_k, dext_v, tuple(grad_ck), tuple(grad_cv), lse[:, 0], delta[:, 0])

def span_pass(items):
    q_span, d_span, ek_span, ev_span, eok_span, ck_span, cv_span, cok_span = items
    mapped = jax.vmap(head_pass, in_axes=(1, 1, 1, 1, None, 1, 1, None), out_axes=1)
    return mapped(q_span, d_span, ek_span, ev_span, eok_span, ck_span, cv_span, cok_span)

def fold_rim(dext, window_span):
    own = dext[:, BLOCK:BLOCK + window_span]
    from_right = shift_spans(dext[:, :BLOCK], -1)
    from_left = shift_spans(dext[:, BLOCK + window_span:], 1)
    filler = jnp.zeros(own.shape[:1] + (window_span - BLOCK,) + own.shape[2:], jnp.float32)
    return own + jnp.concatenate([filler, from_right], axis=1) + jnp.concatenate([from_left, filler], axis=1)

def reference(query, key, value, dout):
    window_span = TOK_DEV
    spans = TOKENS // TOK_DEV
    shape4 = (spans, window_span, HEADS, HEAD_DIM)
    q4 = query.reshape(shape4)
    k4 = key.reshape(shape4)
    v4 = value.reshape(shape4)
    d4 = dout.reshape(shape4)
    index = jnp.arange(spans)

    def extend(x):
        return jnp.concatenate([shift_spans(x, 1)[:, window_span - BLOCK:], x, shift_spans(x, -1)[:, :BLOCK]], axis=1)
    ext_k = extend(k4)
    ext_v = extend(v4)
    ext_ok = jnp.concatenate([jnp.repeat((index > 0)[:, None], BLOCK, axis=1), jnp.ones((spans, window_span), jnp.bool_), jnp.repeat((index < spans - 1)[:, None], BLOCK, axis=1)], axis=1)
    c_keys = []
    c_vals = []
    c_oks = []
    for level in range(LEVELS):
        factor = 2 ** (level + 1)
        size = window_span // factor
        kbar = coarsen(k4, factor)
        vbar = coarsen(v4, factor)
        c_keys.append(jnp.concatenate([shift_spans(kbar, factor), shift_spans(kbar, -factor)], axis=1))
        c_vals.append(jnp.concatenate([shift_spans(vbar, factor), shift_spans(vbar, -factor)], axis=1))
        c_oks.append(jnp.concatenate([jnp.repeat((index >= factor)[:, None], size, axis=1), jnp.repeat((index < spans - factor)[:, None], size, axis=1)], axis=1))
    results = lax.map(span_pass, (q4, d4, ext_k, ext_v, ext_ok, tuple(c_keys), tuple(c_vals), tuple(c_oks)))
    attention_output, query_gradient, dext_k, dext_v, grad_ck, grad_cv, lse, delta = results
    grad_k = fold_rim(dext_k, window_span)
    grad_v = fold_rim(dext_v, window_span)
    for level in range(LEVELS):
        factor = 2 ** (level + 1)
        size = window_span // factor
        part_k = shift_spans(grad_ck[level][:, :size], -factor) + shift_spans(grad_ck[level][:, size:], factor)
        part_v = shift_spans(grad_cv[level][:, :size], -factor) + shift_spans(grad_cv[level][:, size:], factor)
        grad_k = grad_k + jnp.repeat(part_k, factor, axis=1) / factor
        grad_v = grad_v + jnp.repeat(part_v, factor, axis=1) / factor
    shape3 = (TOKENS, HEADS, HEAD_DIM)
    return (attention_output.reshape(shape3), query_gradient.astype(jnp.bfloat16).reshape(shape3), grad_k.astype(jnp.bfloat16).reshape(shape3), grad_v.astype(jnp.bfloat16).reshape(shape3))
```

```python
import functools
import math

import jax
import jax.numpy as jnp
from jax import lax
from jax.experimental import pallas as pl
from jax.experimental.pallas import tpu as pltpu
from jax.sharding import PartitionSpec as P

BLOCK = 256
LEVELS = 3
CHUNKS = 2
LOG2E = math.log2(math.e)

BF = jnp.bfloat16
F32 = jnp.float32


def passed_along(value, steps):
    count = lax.axis_size("seq")
    initial, last = max(0, -steps), min(count, count - steps)
    return lax.ppermute(value, "seq", [(source, source + steps) for source in range(initial, last)])


def nt(left, right):
    return lax.dot_general(left, right, (((1,), (1,)), ((), ())), preferred_element_type=F32)


def nn(left, right):
    return jnp.dot(left, right, preferred_element_type=F32)


def shape(dims, dtype=BF):
    return jax.ShapeDtypeStruct(dims, dtype)


def params():
    return pltpu.CompilerParams(vmem_limit_bytes=48 * 2**20)


def split_kv_kernel(heads, base, k_ref, v_ref, first, last, *rest):
    coarse, (wide, sums) = rest[:LEVELS], rest[LEVELS:]
    per = first.shape[1]
    span = 2 * first.shape[2]
    for at, ref in enumerate((k_ref, v_ref)):
        wide[...] = ref[...].astype(F32)
        for head in range(per):
            row = base + head
            block = span // 2
            first[at, head] = wide[pl.ds(row, block, stride=heads), :].astype(BF)
            last[at, head] = wide[pl.ds(row + heads * block, block, stride=heads), :].astype(BF)
            size = span // 2
            total = (
                wide[pl.ds(row, size, stride=2 * heads), :]
                + wide[pl.ds(row + heads, size, stride=2 * heads), :]
            )
            for level in range(LEVELS):
                coarse[level][at, head] = (total * (1.0 / 2 ** (level + 1))).astype(BF)
                if level + 1 < LEVELS:
                    sums[pl.ds(0, size), :] = total
                    size //= 2
                    total = sums[pl.ds(0, size, stride=2), :] + sums[pl.ds(1, size, stride=2), :]


def split_kv(k2, v2, heads, base, per, span):
    block = span // 2
    outs = [shape((2, per, block, 128)), shape((2, per, block, 128))]
    outs += [shape((2, per, span // 2 ** (level + 1), 128)) for level in range(LEVELS)]
    return pl.pallas_call(
        functools.partial(split_kv_kernel, heads, base),
        out_shape=outs,
        scratch_shapes=[
            pltpu.VMEM((heads * span, 128), F32),
            pltpu.VMEM((span // 2, 128), F32),
        ],
        compiler_params=params(),
        name="split_kv",
        cost_estimate=pl.CostEstimate(flops=0, bytes_accessed=4 * 2**20, transcendentals=0),
    )(k2, v2)


def split_qd_kernel(heads, q_ref, d_ref, q_out, d_out, rep_out, wide, sums, spread):
    span = q_out.shape[1]
    wide[...] = d_ref[...].astype(F32)
    for head in range(heads):
        d_out[head] = wide[pl.ds(head, span, stride=heads), :].astype(BF)
    wide[...] = q_ref[...].astype(F32)
    for head in range(heads):
        q_out[head] = wide[pl.ds(head, span, stride=heads), :].astype(BF)
        size = span // 2
        total = (
            wide[pl.ds(head, size, stride=2 * heads), :]
            + wide[pl.ds(head + heads, size, stride=2 * heads), :]
        )
        for level in range(LEVELS):
            factor = 2 ** (level + 1)
            mean = (total * (1.0 / factor)).astype(BF).astype(F32)
            for row in range(factor):
                spread[pl.ds(row, size, stride=factor), :] = mean
            rep_out[level, head] = spread[...].astype(BF)
            if level + 1 < LEVELS:
                sums[pl.ds(0, size), :] = total
                size //= 2
                total = sums[pl.ds(0, size, stride=2), :] + sums[pl.ds(1, size, stride=2), :]


def split_qd(q2, d2, heads, span):
    return pl.pallas_call(
        functools.partial(split_qd_kernel, heads),
        out_shape=[
            shape((heads, span, 128)),
            shape((heads, span, 128)),
            shape((LEVELS, heads, span, 128)),
        ],
        scratch_shapes=[
            pltpu.VMEM((heads * span, 128), F32),
            pltpu.VMEM((span // 2, 128), F32),
            pltpu.VMEM((span, 128), F32),
        ],
        compiler_params=params(),
        name="split_qd",
        cost_estimate=pl.CostEstimate(flops=0, bytes_accessed=8 * 2**20, transcendentals=0),
    )(q2, d2)


def attend_kernel(
    count, place_ref, q_ref, d_ref, rep_ref, first, last, before, after, *rest
):
    lows, highs = rest[:LEVELS], rest[LEVELS : 2 * LEVELS]
    (att, gq, own, g_before, g_after) = rest[2 * LEVELS : 2 * LEVELS + 5]
    rest = rest[2 * LEVELS + 5 :]
    g_lows, g_highs = rest[:LEVELS], rest[LEVELS : 2 * LEVELS]
    keys, vals, keys_t, vals_t, scores, grads, probs, dscores, rows, total_q = rest[2 * LEVELS :]
    place = place_ref[0]
    block = first.shape[2]
    scale = 1.0 / math.sqrt(128)
    scale2 = scale * LOG2E

    parts = [(before, place > 0, 0), (first, None, 0), (last, None, 0)]
    for level in range(LEVELS):
        factor = 2 ** (level + 1)
        parts.append((lows[level], place >= factor, level + 1))
        parts.append((highs[level], place < count - factor, level + 1))
    parts.append((after, place < count - 1, 0))
    at = 0
    segments = []
    for ref, ok, level in parts:
        size = ref.shape[2]
        keys[pl.ds(at, size), :] = ref[0, 0]
        vals[pl.ds(at, size), :] = ref[1, 0]
        bias = float(level)
        if ok is not None:
            bias = jnp.where(ok, bias, -jnp.inf).astype(F32)
        segments.append((at, size, bias, level))
        at += size
    keys_t[...] = keys[...].T
    vals_t[...] = vals[...].T

    held = None
    for turn in range(2):
        own_rows = pl.ds(turn * block, block)
        q_blk = q_ref[0, own_rows, :]
        d_blk = d_ref[0, own_rows, :]
        using = [q_blk] + [rep_ref[level, 0, own_rows, :] for level in range(LEVELS)]
        mine = segments[:-1] if turn == 0 else segments[1:]
        base = mine[0][0]
        width = mine[-1][0] + mine[-1][1] - base
        top = None
        for start, size, bias, level in mine:
            s = nt(keys[pl.ds(start, size), :], using[level])
            scores[pl.ds(start - base, size), :] = s
            high = jnp.max(s, axis=0, keepdims=True) * scale2 + bias
            top = high if top is None else jnp.maximum(top, high)
        total = jnp.zeros((1, block), F32)
        acc = jnp.zeros((1, block), F32)
        for start, size, bias, level in mine:
            here = pl.ds(start - base, size)
            e = jnp.exp2(scores[here, :] * scale2 - (top - bias))
            scores[here, :] = e
            total = total + jnp.sum(e, axis=0, keepdims=True)
            dp = nt(vals[pl.ds(start, size), :], d_blk)
            grads[here, :] = dp
            acc = acc + jnp.sum(e * dp, axis=0, keepdims=True)
        inverse = 1.0 / total
        delta = acc * inverse
        for start, size, bias, level in mine:
            here = pl.ds(start - base, size)
            p = scores[here, :] * inverse
            probs[here, :] = p.astype(BF)
            dscores[here, :] = (p * (grads[here, :] - delta)).astype(BF)
        att[0, own_rows, :] = nn(vals_t[:, base : base + width], probs[...]).T.astype(BF)
        gv = nn(probs[...], d_blk)
        pieces = {}
        fine = jnp.zeros((128, block), F32)
        for start, size, bias, level in mine:
            here = pl.ds(start - base, size)
            ds = dscores[here, :]
            gk = nn(ds, using[level]) * scale
            pieces[start] = (gk, gv[start - base : start - base + size])
        fine_at = [(s, z) for s, z, _, level in mine if level == 0]
        for start, size in fine_at:
            fine = fine + nn(keys_t[:, start : start + size], dscores[pl.ds(start - base, size), :])
        total_q[...] = fine.T
        for level in range(1, LEVELS + 1):
            spots = [(s, z) for s, z, _, lev in mine if lev == level]
            start, size = spots[0][0], spots[0][1] + spots[1][1]
            up = nn(keys_t[:, start : start + size], dscores[pl.ds(start - base, size), :])
            rows[...] = up.T
            factor = 2**level
            groups = block // factor
            mean = rows[pl.ds(0, groups, stride=factor), :]
            for row in range(1, factor):
                mean = mean + rows[pl.ds(row, groups, stride=factor), :]
            mean = mean * (1.0 / factor)
            for row in range(factor):
                spot = pl.ds(row, groups, stride=factor)
                total_q[spot, :] = total_q[spot, :] + mean
        gq[0, own_rows, :] = (total_q[...] * scale).astype(BF)
        if turn == 0:
            held = pieces
        else:
            for key, pair in pieces.items():
                if key in held:
                    held[key] = (held[key][0] + pair[0], held[key][1] + pair[1])
                else:
                    held[key] = pair

    places = [(g_before, None), (own, 0), (own, block)]
    for level in range(LEVELS):
        places += [(g_lows[level], None), (g_highs[level], None)]
    places.append((g_after, None))
    for (ref, offset), (start, size, bias, level) in zip(places, segments):
        for which in range(2):
            value = held[start][which]
            if offset is None:
                ref[which, 0] = value.astype(ref.dtype)
            else:
                ref[which, 0, pl.ds(offset, size), :] = value


def attend(place, count, q, d, rep, base, first, last, before, after, lows, highs):
    per, block = first.shape[1], first.shape[2]
    span = 2 * block
    sizes = [x.shape[2] for x in lows]
    columns = 4 * block + 2 * sum(sizes)
    width = columns - block

    def pair(size):
        return pl.BlockSpec((2, 1, size, 128), lambda h: (0, h, 0, 0))

    head_in = pl.BlockSpec((1, span, 128), lambda h: (base + h, 0, 0))
    head_out = pl.BlockSpec((1, span, 128), lambda h: (h, 0, 0))
    flops = 2 * per * span * width * 128 * 6
    return pl.pallas_call(
        functools.partial(attend_kernel, count),
        grid=(per,),
        in_specs=[
            pl.BlockSpec(memory_space=pltpu.SMEM),
            head_in,
            head_in,
            pl.BlockSpec((LEVELS, 1, span, 128), lambda h: (0, base + h, 0, 0)),
        ]
        + [pair(block)] * 4
        + [pair(size) for size in sizes] * 2,
        out_specs=[head_out, head_out, pair(span), pair(block), pair(block)]
        + [pair(size) for size in sizes] * 2,
        out_shape=[
            shape((per, span, 128)),
            shape((per, span, 128)),
            shape((2, per, span, 128), F32),
            shape((2, per, block, 128)),
            shape((2, per, block, 128)),
        ]
        + [shape((2, per, size, 128)) for size in sizes] * 2,
        scratch_shapes=[
            pltpu.VMEM((columns, 128), BF),
            pltpu.VMEM((columns, 128), BF),
            pltpu.VMEM((128, columns), BF),
            pltpu.VMEM((128, columns), BF),
            pltpu.VMEM((width, block), F32),
            pltpu.VMEM((width, block), F32),
            pltpu.VMEM((width, block), BF),
            pltpu.VMEM((width, block), BF),
            pltpu.VMEM((block, 128), F32),
            pltpu.VMEM((block, 128), F32),
        ],
        compiler_params=params(),
        name="attend",
        cost_estimate=pl.CostEstimate(
            flops=flops, bytes_accessed=8 * 2**20, transcendentals=per * span * width
        ),
    )(place, q, d, rep, first, last, before, after, *lows, *highs)


def join_kernel(heads, *refs):
    ins, (wide,) = refs[: 2 * CHUNKS], refs[-1:]
    outs = refs[2 * CHUNKS : 2 * CHUNKS + 2]
    per, span = ins[0].shape[0], ins[0].shape[1]
    for which in range(2):
        for chunk in range(CHUNKS):
            for head in range(per):
                wide[pl.ds(chunk * per + head, span, stride=heads), :] = ins[
                    which * CHUNKS + chunk
                ][head].astype(F32)
        outs[which][...] = wide[...].astype(BF)


def join(atts, gqs, heads, span):
    return pl.pallas_call(
        functools.partial(join_kernel, heads),
        out_shape=[shape((heads * span, 128))] * 2,
        scratch_shapes=[pltpu.VMEM((heads * span, 128), F32)],
        compiler_params=params(),
        name="join",
        cost_estimate=pl.CostEstimate(flops=0, bytes_accessed=4 * 2**20, transcendentals=0),
    )(*atts, *gqs)


def gather_kernel(heads, *refs):
    width = 3 + 2 * LEVELS
    groups = [refs[chunk * width : (chunk + 1) * width] for chunk in range(CHUNKS)]
    outs = refs[CHUNKS * width : CHUNKS * width + 2]
    wide, part, mine = refs[CHUNKS * width + 2 :]
    for which in range(2):
        for chunk, group in enumerate(groups):
            own, right, left = group[:3]
            downs, ups = group[3 : 3 + LEVELS], group[3 + LEVELS :]
            per, span = own.shape[1], own.shape[2]
            block = span // 2
            for head in range(per):
                carry = None
                for level in reversed(range(LEVELS)):
                    size = span // 2 ** (level + 1)
                    value = (
                        downs[level][which, head].astype(F32) + ups[level][which, head].astype(F32)
                    ) * (1.0 / 2 ** (level + 1))
                    if carry is not None:
                        half = size // 2
                        part[pl.ds(0, half, stride=2), :] = carry
                        part[pl.ds(1, half, stride=2), :] = carry
                        value = value + part[pl.ds(0, size), :]
                    carry = value
                mine[pl.ds(0, block), :] = own[which, head, :block] + left[which, head].astype(F32)
                mine[pl.ds(block, block), :] = own[which, head, block:] + right[which, head].astype(
                    F32
                )
                row = chunk * per + head
                for odd in range(2):
                    wide[pl.ds(row + heads * odd, block, stride=2 * heads), :] = (
                        mine[pl.ds(odd, block, stride=2), :] + carry
                    )
        outs[which][...] = wide[...].astype(BF)


def gather(groups, heads, span):
    return pl.pallas_call(
        functools.partial(gather_kernel, heads),
        out_shape=[shape((heads * span, 128))] * 2,
        scratch_shapes=[
            pltpu.VMEM((heads * span, 128), F32),
            pltpu.VMEM((span // 2, 128), F32),
            pltpu.VMEM((span, 128), F32),
        ],
        compiler_params=params(),
        name="gather",
        cost_estimate=pl.CostEstimate(flops=0, bytes_accessed=8 * 2**20, transcendentals=0),
    )(*[x for group in groups for x in group])


def local(query, key, value, dout):
    span, heads, width = query.shape
    per = heads // CHUNKS
    count = lax.axis_size("seq")
    place = jnp.reshape(lax.axis_index("seq"), (1,)).astype(jnp.int32)
    flat = (heads * span, width)
    q2, k2, v2, d2 = (x.reshape(flat) for x in (query, key, value, dout))
    sent = []
    for chunk in range(CHUNKS):
        first, last, *coarse = split_kv(k2, v2, heads, chunk * per, per, span)
        before = passed_along(last, 1)
        after = passed_along(first, -1)
        lows = [passed_along(x, 2 ** (level + 1)) for level, x in enumerate(coarse)]
        highs = [passed_along(x, -(2 ** (level + 1))) for level, x in enumerate(coarse)]
        sent.append((first, last, before, after, lows, highs))
    qh, dh, rep = split_qd(q2, d2, heads, span)
    atts, gqs, groups = [], [], []
    for chunk in range(CHUNKS):
        att, gq, own, g_before, g_after, *grads = attend(
            place, count, qh, dh, rep, chunk * per, *sent[chunk]
        )
        atts.append(att)
        gqs.append(gq)
        right = passed_along(g_before, -1)
        left = passed_along(g_after, 1)
        downs = [passed_along(x, -(2 ** (level + 1))) for level, x in enumerate(grads[:LEVELS])]
        ups = [passed_along(x, 2 ** (level + 1)) for level, x in enumerate(grads[LEVELS:])]
        groups.append([own, right, left, *downs, *ups])
    attended, grad_query = join(atts, gqs, heads, span)
    grad_key, grad_value = gather(groups, heads, span)
    return tuple(
        x.reshape(span, heads, width) for x in (attended, grad_query, grad_key, grad_value)
    )


def solution(mesh):
    placed = P("seq", "head", None)
    return jax.shard_map(
        local,
        mesh=mesh,
        in_specs=(placed,) * 4,
        out_specs=(placed,) * 4,
        check_vma=False,
    )
```

```python
import functools
import math

import jax
import jax.numpy as jnp
from jax import lax
from jax.experimental import pallas as pl
from jax.experimental.pallas import tpu as pltpu
from jax.sharding import PartitionSpec as P

BLOCK = 256
LEVELS = 3
LOG2E = math.log2(math.e)

BF = jnp.bfloat16
F32 = jnp.float32


def crossed(value, steps):
    count = lax.axis_size("seq")
    pairs = [(at, at + (steps if at % 2 == 0 else -steps)) for at in range(count)]
    return lax.ppermute(value, "seq", [(at, to) for at, to in pairs if 0 <= to < count])


def swapped(value):
    count = lax.axis_size("seq")
    return lax.ppermute(value, "seq", [(at, at ^ 1) for at in range(count)])


def nt(left, right):
    return lax.dot_general(left, right, (((1,), (1,)), ((), ())), preferred_element_type=F32)


def nn(left, right):
    return jnp.dot(left, right, preferred_element_type=F32)


def shape(dims, dtype=BF):
    return jax.ShapeDtypeStruct(dims, dtype)


def params(mib):
    return pltpu.CompilerParams(vmem_limit_bytes=mib * 2**20)


SMEM_SPEC = pl.BlockSpec(memory_space=pltpu.SMEM)
VMEM_SPEC = pl.BlockSpec(memory_space=pltpu.VMEM)


def turned(wide, ref, odd):
    half = wide.shape[0] // 2
    wide[pl.ds(pl.multiple_of(odd * half, half), half), :] = ref[:half].astype(F32)
    wide[pl.ds(pl.multiple_of((1 - odd) * half, half), half), :] = ref[half:].astype(F32)


def turned_back(ref, wide, odd):
    half = wide.shape[0] // 2
    ref[pl.ds(pl.multiple_of(odd * half, half), half), :] = wide[:half].astype(BF)
    ref[pl.ds(pl.multiple_of((1 - odd) * half, half), half), :] = wide[half:].astype(BF)


def pair_sums(wide, row, size, heads):
    return (
        wide[pl.ds(row, size, stride=2 * heads), :]
        + wide[pl.ds(row + heads, size, stride=2 * heads), :]
    )


def next_sums(sums, total):
    size = total.shape[0]
    sums[pl.ds(0, size), :] = total
    half = size // 2
    return sums[pl.ds(0, half, stride=2), :] + sums[pl.ds(1, half, stride=2), :]


def split_kv_kernel(heads, place_ref, k_ref, v_ref, outer, inner, *rest):
    coarse, (wide, sums) = rest[:LEVELS], rest[LEVELS:]
    block = inner.shape[2]
    odd = lax.rem(place_ref[0], 2)
    for at, ref in enumerate((k_ref, v_ref)):
        turned(wide, ref, odd)
        for head in range(heads):
            outer[2 + at, head] = wide[pl.ds(head, block, stride=heads), :].astype(BF)
            inner[at, head] = wide[pl.ds(head + heads * block, block, stride=heads), :].astype(BF)
            total = pair_sums(wide, head, block, heads)
            for level in range(LEVELS):
                mean = (total * (1.0 / 2 ** (level + 1))).astype(BF)
                coarse[level][at, head] = mean
                if level == 0:
                    outer[at, head] = mean
                if level + 1 < LEVELS:
                    total = next_sums(sums, total)


def split_kv(place, k2, v2, heads, span):
    block = span // 2
    outs = [shape((4, heads, block, 128)), shape((2, heads, block, 128))]
    outs += [shape((2, heads, span // 2 ** (level + 1), 128)) for level in range(LEVELS)]
    return pl.pallas_call(
        functools.partial(split_kv_kernel, heads),
        out_shape=outs,
        in_specs=[SMEM_SPEC, VMEM_SPEC, VMEM_SPEC],
        scratch_shapes=[
            pltpu.VMEM((heads * span, 128), F32),
            pltpu.VMEM((block, 128), F32),
        ],
        compiler_params=params(16),
        name="split_kv",
        cost_estimate=pl.CostEstimate(flops=0, bytes_accessed=4 * 2**20, transcendentals=0),
    )(place, k2, v2)


def relay_kernel(near, inner, *refs):
    refs[-1][:2] = near[2:]
    refs[-1][2:] = inner[...]


def relay(near, inner, earlier):
    return pl.pallas_call(
        relay_kernel,
        out_shape=shape(near.shape),
        in_specs=[VMEM_SPEC] * 2 + [pl.BlockSpec(memory_space=pl.ANY)] * len(earlier),
        compiler_params=params(8),
        name="relay",
        cost_estimate=pl.CostEstimate(flops=0, bytes_accessed=2 * 2**20, transcendentals=0),
    )(near, inner, *earlier)


def split_qd_kernel(heads, place_ref, q_ref, d_ref, q_out, d_out, rep_out, wide, sums, spread):
    span = q_out.shape[1]
    odd = lax.rem(place_ref[0], 2)
    turned(wide, d_ref, odd)
    for head in range(heads):
        d_out[head] = wide[pl.ds(head, span, stride=heads), :].astype(BF)
    turned(wide, q_ref, odd)
    for head in range(heads):
        q_out[head] = wide[pl.ds(head, span, stride=heads), :].astype(BF)
        total = pair_sums(wide, head, span // 2, heads)
        for level in range(LEVELS):
            factor = 2 ** (level + 1)
            mean = (total * (1.0 / factor)).astype(BF).astype(F32)
            for row in range(factor):
                spread[pl.ds(row, span // factor, stride=factor), :] = mean
            rep_out[level, head] = spread[...].astype(BF)
            if level + 1 < LEVELS:
                total = next_sums(sums, total)


def split_qd(place, q2, d2, heads, span):
    return pl.pallas_call(
        functools.partial(split_qd_kernel, heads),
        out_shape=[
            shape((heads, span, 128)),
            shape((heads, span, 128)),
            shape((LEVELS, heads, span, 128)),
        ],
        in_specs=[SMEM_SPEC] + [VMEM_SPEC] * 2,
        scratch_shapes=[
            pltpu.VMEM((heads * span, 128), F32),
            pltpu.VMEM((span // 2, 128), F32),
            pltpu.VMEM((span, 128), F32),
        ],
        compiler_params=params(16),
        name="split_qd",
        cost_estimate=pl.CostEstimate(flops=0, bytes_accessed=8 * 2**20, transcendentals=0),
    )(place, q2, d2)


def attend_kernel(count, place_ref, q_ref, d_ref, rep_ref, outer, inner, rim_out, rim_in, *rest):
    crossed_a, crossed_b = rest[:LEVELS], rest[LEVELS : 2 * LEVELS]
    att, gq, own, g_rims = rest[2 * LEVELS : 2 * LEVELS + 4]
    rest = rest[2 * LEVELS + 4 :]
    g_as, g_bs = rest[:LEVELS], rest[LEVELS : 2 * LEVELS]
    keys, vals, keys_t, vals_t, scores, grads, probs, dscores, rows, total_q = rest[2 * LEVELS :]
    place = place_ref[0]
    even = lax.rem(place, 2) == 0
    block = outer.shape[2]
    scale = 1.0 / math.sqrt(128)
    scale2 = scale * LOG2E

    def reaches(below, steps):
        return jnp.where(below, place >= steps, place < count - steps)

    parts = [(rim_out, reaches(even, 1), 0), (outer, None, 0), (inner, None, 0)]
    for level in range(LEVELS):
        factor = 2 ** (level + 1)
        parts.append((crossed_a[level], reaches(even, factor), level + 1))
        parts.append((crossed_b[level], reaches(jnp.logical_not(even), factor), level + 1))
    parts.append((rim_in, None, 0))
    at = 0
    segments = []
    for ref, ok, level in parts:
        size = ref.shape[2]
        keys[pl.ds(at, size), :] = ref[0, 0]
        vals[pl.ds(at, size), :] = ref[1, 0]
        bias = float(level)
        if ok is not None:
            bias = jnp.where(ok, bias, -jnp.inf).astype(F32)
        segments.append((at, size, bias, level))
        at += size
    keys_t[...] = keys[...].T
    vals_t[...] = vals[...].T

    held = None
    for turn in range(2):
        own_rows = pl.ds(turn * block, block)
        q_blk = q_ref[0, own_rows, :]
        d_blk = d_ref[0, own_rows, :]
        using = [q_blk] + [rep_ref[level, 0, own_rows, :] for level in range(LEVELS)]
        mine = segments[:-1] if turn == 0 else segments[1:]
        base = mine[0][0]
        width = mine[-1][0] + mine[-1][1] - base
        top = None
        for start, size, bias, level in mine:
            s = nt(keys[pl.ds(start, size), :], using[level])
            scores[pl.ds(start - base, size), :] = s
            high = jnp.max(s, axis=0, keepdims=True) * scale2 + bias
            top = high if top is None else jnp.maximum(top, high)
        total = jnp.zeros((1, block), F32)
        acc = jnp.zeros((1, block), F32)
        for start, size, bias, level in mine:
            here = pl.ds(start - base, size)
            e = jnp.exp2(scores[here, :] * scale2 - (top - bias))
            scores[here, :] = e
            total = total + jnp.sum(e, axis=0, keepdims=True)
            dp = nt(vals[pl.ds(start, size), :], d_blk)
            grads[here, :] = dp
            acc = acc + jnp.sum(e * dp, axis=0, keepdims=True)
        inverse = 1.0 / total
        delta = acc * inverse
        for start, size, bias, level in mine:
            here = pl.ds(start - base, size)
            p = scores[here, :] * inverse
            probs[here, :] = p.astype(BF)
            dscores[here, :] = (p * (grads[here, :] - delta)).astype(BF)
        att[0, own_rows, :] = nn(vals_t[:, base : base + width], probs[...]).T.astype(BF)
        gv = nn(probs[...], d_blk)
        pieces = {}
        fine = jnp.zeros((128, block), F32)
        for start, size, bias, level in mine:
            here = pl.ds(start - base, size)
            ds = dscores[here, :]
            gk = nn(ds, using[level]) * scale
            pieces[start] = (gk, gv[start - base : start - base + size])
        fine_at = [(s, z) for s, z, _, level in mine if level == 0]
        for start, size in fine_at:
            fine = fine + nn(keys_t[:, start : start + size], dscores[pl.ds(start - base, size), :])
        total_q[...] = fine.T
        for level in range(1, LEVELS + 1):
            spots = [(s, z) for s, z, _, lev in mine if lev == level]
            start, size = spots[0][0], spots[0][1] + spots[1][1]
            up = nn(keys_t[:, start : start + size], dscores[pl.ds(start - base, size), :])
            rows[...] = up.T
            factor = 2**level
            groups = block // factor
            mean = rows[pl.ds(0, groups, stride=factor), :]
            for row in range(1, factor):
                mean = mean + rows[pl.ds(row, groups, stride=factor), :]
            mean = mean * (1.0 / factor)
            for row in range(factor):
                spot = pl.ds(row, groups, stride=factor)
                total_q[spot, :] = total_q[spot, :] + mean
        gq[0, own_rows, :] = (total_q[...] * scale).astype(BF)
        if turn == 0:
            held = pieces
        else:
            for key, pair in pieces.items():
                if key in held:
                    held[key] = (held[key][0] + pair[0], held[key][1] + pair[1])
                else:
                    held[key] = pair

    places = [(g_rims, 0, None), (own, 0, 0), (own, 0, block)]
    for level in range(LEVELS):
        places += [(g_as[level], 0, None), (g_bs[level], 0, None)]
    places.append((g_rims, 2, None))
    for (ref, lead, offset), (start, size, bias, level) in zip(places, segments):
        for which in range(2):
            value = held[start][which]
            if offset is None:
                ref[lead + which, 0] = value.astype(ref.dtype)
            else:
                ref[which, 0, pl.ds(offset, size), :] = value


def attend(place, count, q, d, rep, outer, inner, rims, crossed_a, crossed_b):
    heads, block = inner.shape[1], inner.shape[2]
    span = 2 * block
    sizes = [span // 2 ** (level + 1) for level in range(LEVELS)]
    columns = 4 * block + 2 * sum(sizes)
    width = columns - block

    def pair(size, at=0):
        return pl.BlockSpec((2, 1, size, 128), lambda h: (at, h, 0, 0))

    head_spec = pl.BlockSpec((1, span, 128), lambda h: (h, 0, 0))
    flops = 2 * heads * span * width * 128 * 6
    return pl.pallas_call(
        functools.partial(attend_kernel, count),
        grid=(heads,),
        in_specs=[
            SMEM_SPEC,
            head_spec,
            head_spec,
            pl.BlockSpec((LEVELS, 1, span, 128), lambda h: (0, h, 0, 0)),
            pair(block, 1),
            pair(block),
            pair(block, 0),
            pair(block, 1),
        ]
        + [pair(size) for size in sizes] * 2,
        out_specs=[
            head_spec,
            head_spec,
            pair(span),
            pl.BlockSpec((4, 1, block, 128), lambda h: (0, h, 0, 0)),
        ]
        + [pair(size) for size in sizes] * 2,
        out_shape=[
            shape((heads, span, 128)),
            shape((heads, span, 128)),
            shape((2, heads, span, 128), F32),
            shape((4, heads, block, 128)),
        ]
        + [shape((2, heads, size, 128)) for size in sizes] * 2,
        scratch_shapes=[
            pltpu.VMEM((columns, 128), BF),
            pltpu.VMEM((columns, 128), BF),
            pltpu.VMEM((128, columns), BF),
            pltpu.VMEM((128, columns), BF),
            pltpu.VMEM((width, block), F32),
            pltpu.VMEM((width, block), F32),
            pltpu.VMEM((width, block), BF),
            pltpu.VMEM((width, block), BF),
            pltpu.VMEM((block, 128), F32),
            pltpu.VMEM((block, 128), F32),
        ],
        compiler_params=params(24),
        name="attend",
        cost_estimate=pl.CostEstimate(
            flops=flops, bytes_accessed=8 * 2**20, transcendentals=heads * span * width
        ),
    )(place, q, d, rep, outer, inner, rims, rims, *crossed_a, *crossed_b)


def merge_kernel(count, *refs):
    coarse, fine, tails = refs[:count], refs[count : 2 * count], refs[2 * count : -count - 1]
    outs, wide = refs[-count - 1 : -1], refs[-1]
    for at in range(count):
        rows = fine[at].shape[0]
        half = coarse[at][...].astype(F32) * 0.5
        wide[pl.ds(0, rows // 2, stride=2), :] = half
        wide[pl.ds(1, rows // 2, stride=2), :] = half
        outs[at][:rows] = (wide[...] + fine[at][...].astype(F32)).astype(BF)
    for at, tail in enumerate(tails):
        rows = fine[count - 1].shape[0]
        outs[count - 1][rows:] = tail[: outs[count - 1].shape[0] - rows]


def merge(coarse, fine, tail=None):
    def flat(x):
        return x.reshape(-1, 128)

    heads, size = fine[0].shape[1], fine[0].shape[2]
    rows = 2 * heads * size
    dims = [(2, heads, size, 128)] * 2
    extra = []
    if tail is not None:
        dims[1] = (4, heads, size, 128)
        extra = [flat(tail)]
    outs = pl.pallas_call(
        functools.partial(merge_kernel, 2),
        out_shape=[shape((math.prod(x[:3]), 128)) for x in dims],
        scratch_shapes=[pltpu.VMEM((rows, 128), F32)],
        compiler_params=params(12),
        name="merge",
        cost_estimate=pl.CostEstimate(flops=0, bytes_accessed=2 * 2**20, transcendentals=0),
    )(*map(flat, coarse), *map(flat, fine), *extra)
    return [x.reshape(dim) for x, dim in zip(outs, dims)]


def join_kernel(heads, place_ref, att, gq, att_out, gq_out, wide):
    span = att.shape[1]
    odd = lax.rem(place_ref[0], 2)
    for ref, out in ((att, att_out), (gq, gq_out)):
        for head in range(heads):
            wide[pl.ds(head, span, stride=heads), :] = ref[head].astype(F32)
        turned_back(out, wide, odd)


def join(place, att, gq):
    heads, span = att.shape[:2]
    return pl.pallas_call(
        functools.partial(join_kernel, heads),
        out_shape=[shape((heads * span, 128))] * 2,
        in_specs=[SMEM_SPEC, VMEM_SPEC, VMEM_SPEC],
        scratch_shapes=[pltpu.VMEM((heads * span, 128), F32)],
        compiler_params=params(12),
        name="join",
        cost_estimate=pl.CostEstimate(flops=0, bytes_accessed=4 * 2**20, transcendentals=0),
    )(place, att, gq)


def gather_kernel(heads, place_ref, own, rims, coarse_a, coarse_b, gk_out, gv_out, wide, mine):
    span = own.shape[2]
    block = span // 2
    odd = lax.rem(place_ref[0], 2)
    for which, out in enumerate((gk_out, gv_out)):
        for head in range(heads):
            spread = (
                coarse_a[which, head].astype(F32) + coarse_b[which, head].astype(F32)
            ) * 0.5
            outer, inner = coarse_b[2 + which, head], rims[2 + which, head]
            mine[pl.ds(0, block), :] = own[which, head, :block] + outer.astype(F32)
            mine[pl.ds(block, block), :] = own[which, head, block:] + inner.astype(F32)
            for second in range(2):
                wide[pl.ds(head + heads * second, block, stride=2 * heads), :] = (
                    mine[pl.ds(second, block, stride=2), :] + spread
                )
        turned_back(out, wide, odd)


def gather(place, own, rims, coarse_a, coarse_b):
    heads, span = own.shape[1:3]
    return pl.pallas_call(
        functools.partial(gather_kernel, heads),
        out_shape=[shape((heads * span, 128))] * 2,
        in_specs=[SMEM_SPEC] + [VMEM_SPEC] * 4,
        scratch_shapes=[
            pltpu.VMEM((heads * span, 128), F32),
            pltpu.VMEM((span, 128), F32),
        ],
        compiler_params=params(16),
        name="gather",
        cost_estimate=pl.CostEstimate(flops=0, bytes_accessed=8 * 2**20, transcendentals=0),
    )(place, own, rims, coarse_a, coarse_b)


def local(query, key, value, dout):
    span, heads, width = query.shape
    count = lax.axis_size("seq")
    place = jnp.reshape(lax.axis_index("seq"), (1,)).astype(jnp.int32)
    flat = (heads * span, width)
    q2, k2, v2, d2 = (x.reshape(flat) for x in (query, key, value, dout))
    outer, inner, *coarse = split_kv(place, k2, v2, heads, span)
    near_b = crossed(outer, -2)
    near_a = crossed(coarse[0], 2)
    crossed_a = [near_a] + [crossed(coarse[level], 2 ** (level + 1)) for level in (1, 2)]
    crossed_b = [near_b] + [crossed(coarse[level], -(2 ** (level + 1))) for level in (1, 2)]
    qh, dh, rep = split_qd(place, q2, d2, heads, span)
    rims = swapped(relay(near_b, inner, [near_a, crossed_a[1], crossed_b[1]]))
    att, gq, own, g_rims, *grads = attend(
        place, count, qh, dh, rep, outer, inner, rims, crossed_a, crossed_b
    )
    g_as, g_bs = grads[:LEVELS], grads[LEVELS:]
    far_a, far_b = crossed(g_as[2], -4), crossed(g_bs[2], 4)
    g_rims = swapped(g_rims)
    mid_a, mid_b = merge((far_a, far_b), (g_as[1], g_bs[1]))
    mid_a, mid_b = crossed(mid_a, -2), crossed(mid_b, 2)
    last_a, last_b = merge((mid_a, mid_b), (g_as[0], g_bs[0]), g_rims)
    last_a, last_b = crossed(last_a, -2), crossed(last_b, 2)
    attended, grad_query = join(place, att, gq)
    grad_key, grad_value = gather(place, own, g_rims, last_a, last_b)
    return tuple(
        x.reshape(span, heads, width) for x in (attended, grad_query, grad_key, grad_value)
    )


def solution(mesh):
    placed = P("seq", "head", None)
    return jax.shard_map(
        local,
        mesh=mesh,
        in_specs=(placed,) * 4,
        out_specs=(placed,) * 4,
        check_vma=False,
    )
```

```python
import functools
import math

import jax
import jax.numpy as jnp
from jax import lax
from jax.experimental import pallas as pl
from jax.experimental.pallas import tpu as pltpu
from jax.sharding import PartitionSpec as P

BLOCK = 256
LEVELS = 3
LOG2E = math.log2(math.e)

BF = jnp.bfloat16
F32 = jnp.float32


def crossed(value, steps):
    count = lax.axis_size("seq")
    pairs = [(at, at + (steps if at % 2 == 0 else -steps)) for at in range(count)]
    return lax.ppermute(value, "seq", [(at, to) for at, to in pairs if 0 <= to < count])


def swapped(value, across):
    count = lax.axis_size("seq")
    pairs = [(at, at ^ 1) for at in range(count)]
    if across:
        pairs = [(at, at + 1 if at % 2 else at - 1) for at in range(count)]
    return lax.ppermute(value, "seq", [(at, to) for at, to in pairs if 0 <= to < count])


def nt(left, right):
    return lax.dot_general(left, right, (((1,), (1,)), ((), ())), preferred_element_type=F32)


def nn(left, right):
    return jnp.dot(left, right, preferred_element_type=F32)


def shape(dims, dtype=BF):
    return jax.ShapeDtypeStruct(dims, dtype)


def params(mib):
    return pltpu.CompilerParams(vmem_limit_bytes=mib * 2**20)


SMEM_SPEC = pl.BlockSpec(memory_space=pltpu.SMEM)
VMEM_SPEC = pl.BlockSpec(memory_space=pltpu.VMEM)


def turned(wide, ref, odd):
    half = wide.shape[0] // 2
    wide[pl.ds(pl.multiple_of(odd * half, half), half), :] = ref[:half].astype(F32)
    wide[pl.ds(pl.multiple_of((1 - odd) * half, half), half), :] = ref[half:].astype(F32)


def turned_back(ref, wide, odd):
    half = wide.shape[0] // 2
    ref[pl.ds(pl.multiple_of(odd * half, half), half), :] = wide[:half].astype(BF)
    ref[pl.ds(pl.multiple_of((1 - odd) * half, half), half), :] = wide[half:].astype(BF)


def pair_sums(wide, row, size, heads):
    return (
        wide[pl.ds(row, size, stride=2 * heads), :]
        + wide[pl.ds(row + heads, size, stride=2 * heads), :]
    )


def next_sums(sums, total):
    size = total.shape[0]
    sums[pl.ds(0, size), :] = total
    half = size // 2
    return sums[pl.ds(0, half, stride=2), :] + sums[pl.ds(1, half, stride=2), :]


def split_kv_kernel(heads, place_ref, k_ref, v_ref, outer, inner, *rest):
    coarse, (wide, sums) = rest[:LEVELS], rest[LEVELS:]
    block = inner.shape[2]
    odd = lax.rem(place_ref[0], 2)
    for at, ref in enumerate((k_ref, v_ref)):
        turned(wide, ref, odd)
        for head in range(heads):
            outer[at, head] = wide[pl.ds(head, block, stride=heads), :].astype(BF)
            inner[at, head] = wide[pl.ds(head + heads * block, block, stride=heads), :].astype(BF)
            total = pair_sums(wide, head, block, heads)
            for level in range(LEVELS):
                coarse[level][at, head] = (total * (1.0 / 2 ** (level + 1))).astype(BF)
                if level + 1 < LEVELS:
                    total = next_sums(sums, total)


def split_kv(place, k2, v2, heads, span):
    block = span // 2
    outs = [shape((2, heads, block, 128))] * 2
    outs += [shape((2, heads, span // 2 ** (level + 1), 128)) for level in range(LEVELS)]
    return pl.pallas_call(
        functools.partial(split_kv_kernel, heads),
        out_shape=outs,
        in_specs=[SMEM_SPEC, VMEM_SPEC, VMEM_SPEC],
        scratch_shapes=[
            pltpu.VMEM((heads * span, 128), F32),
            pltpu.VMEM((block, 128), F32),
        ],
        compiler_params=params(16),
        name="split_kv",
        cost_estimate=pl.CostEstimate(flops=0, bytes_accessed=4 * 2**20, transcendentals=0),
    )(place, k2, v2)


def later_kernel(count, *refs):
    for at in range(count):
        refs[len(refs) - count + at][...] = refs[at][...]


def later(after, arrays):
    return pl.pallas_call(
        functools.partial(later_kernel, len(arrays)),
        out_shape=[shape(x.shape) for x in arrays],
        in_specs=[VMEM_SPEC] * len(arrays) + [pl.BlockSpec(memory_space=pl.ANY)] * len(after),
        compiler_params=params(8),
        name="later",
        cost_estimate=pl.CostEstimate(flops=0, bytes_accessed=2 * 2**20, transcendentals=0),
    )(*arrays, *after)


def exchange(firsts, seconds, outer, inner):
    steps = [2 ** (level + 1) for level in range(LEVELS)]
    down = [crossed(x, -step) for x, step in zip(firsts, steps)]
    rims = swapped(outer, True), swapped(inner, False)
    up = [
        crossed(x, step) for x, step in zip(later((*down[1:], rims[1]), seconds), steps)
    ]
    return down, up, rims


def split_qd_kernel(heads, place_ref, q_ref, d_ref, q_out, d_out, rep_out, wide, sums, spread):
    span = q_out.shape[1]
    odd = lax.rem(place_ref[0], 2)
    turned(wide, d_ref, odd)
    for head in range(heads):
        d_out[head] = wide[pl.ds(head, span, stride=heads), :].astype(BF)
    turned(wide, q_ref, odd)
    for head in range(heads):
        q_out[head] = wide[pl.ds(head, span, stride=heads), :].astype(BF)
        total = pair_sums(wide, head, span // 2, heads)
        for level in range(LEVELS):
            factor = 2 ** (level + 1)
            mean = (total * (1.0 / factor)).astype(BF).astype(F32)
            for row in range(factor):
                spread[pl.ds(row, span // factor, stride=factor), :] = mean
            rep_out[level, head] = spread[...].astype(BF)
            if level + 1 < LEVELS:
                total = next_sums(sums, total)


def split_qd(place, q2, d2, heads, span):
    return pl.pallas_call(
        functools.partial(split_qd_kernel, heads),
        out_shape=[
            shape((heads, span, 128)),
            shape((heads, span, 128)),
            shape((LEVELS, heads, span, 128)),
        ],
        in_specs=[SMEM_SPEC] + [VMEM_SPEC] * 2,
        scratch_shapes=[
            pltpu.VMEM((heads * span, 128), F32),
            pltpu.VMEM((span // 2, 128), F32),
            pltpu.VMEM((span, 128), F32),
        ],
        compiler_params=params(16),
        name="split_qd",
        cost_estimate=pl.CostEstimate(flops=0, bytes_accessed=8 * 2**20, transcendentals=0),
    )(place, q2, d2)


def attend_kernel(count, place_ref, q_ref, d_ref, rep_ref, outer, inner, rim_out, rim_in, *rest):
    crossed_a, crossed_b = rest[:LEVELS], rest[LEVELS : 2 * LEVELS]
    att, gq, own, g_out, g_in = rest[2 * LEVELS : 2 * LEVELS + 5]
    rest = rest[2 * LEVELS + 5 :]
    g_as, g_bs = rest[:LEVELS], rest[LEVELS : 2 * LEVELS]
    keys, vals, keys_t, vals_t, scores, grads, probs, dscores, rows, total_q = rest[2 * LEVELS :]
    place = place_ref[0]
    even = lax.rem(place, 2) == 0
    block = outer.shape[2]
    scale = 1.0 / math.sqrt(128)
    scale2 = scale * LOG2E

    def reaches(below, steps):
        return jnp.where(below, place >= steps, place < count - steps)

    parts = [(rim_out, reaches(even, 1), 0), (outer, None, 0), (inner, None, 0)]
    for level in range(LEVELS):
        factor = 2 ** (level + 1)
        parts.append((crossed_a[level], reaches(even, factor), level + 1))
        parts.append((crossed_b[level], reaches(jnp.logical_not(even), factor), level + 1))
    parts.append((rim_in, None, 0))
    at = 0
    segments = []
    for ref, ok, level in parts:
        size = ref.shape[2]
        keys[pl.ds(at, size), :] = ref[0, 0]
        vals[pl.ds(at, size), :] = ref[1, 0]
        bias = float(level)
        if ok is not None:
            bias = jnp.where(ok, bias, -jnp.inf).astype(F32)
        segments.append((at, size, bias, level))
        at += size
    columns = at
    keys_t[...] = keys[...].T
    vals_t[...] = vals[...].T

    turns = (0, 1)
    cols = [pl.ds(turn * block, block) for turn in turns]
    met = [segments[:-1], segments[1:]]
    top = [None, None]
    for turn in turns:
        d_blk = d_ref[0, cols[turn], :]
        using = [q_ref[0, cols[turn], :]]
        using += [rep_ref[level, 0, cols[turn], :] for level in range(LEVELS)]
        for start, size, bias, level in met[turn]:
            here = pl.ds(start, size)
            s = nt(keys[here, :], using[level])
            scores[turn, here, :] = s
            high = jnp.max(s, axis=0, keepdims=True) * scale2 + bias
            top[turn] = high if top[turn] is None else jnp.maximum(top[turn], high)
            grads[turn, here, :] = nt(vals[here, :], d_blk)
    inverse, delta = [None, None], [None, None]
    for turn in turns:
        total = jnp.zeros((1, block), F32)
        acc = jnp.zeros((1, block), F32)
        for start, size, bias, level in met[turn]:
            here = pl.ds(start, size)
            e = jnp.exp2(scores[turn, here, :] * scale2 - (top[turn] - bias))
            scores[turn, here, :] = e
            total = total + jnp.sum(e, axis=0, keepdims=True)
            acc = acc + jnp.sum(e * grads[turn, here, :], axis=0, keepdims=True)
        inverse[turn] = 1.0 / total
        delta[turn] = acc * inverse[turn]
    for turn in turns:
        for start, size, bias, level in met[turn]:
            here = pl.ds(start, size)
            p = scores[turn, here, :] * inverse[turn]
            probs[here, cols[turn]] = p.astype(BF)
            dscores[here, cols[turn]] = (p * (grads[turn, here, :] - delta[turn])).astype(BF)
        first, last = met[turn][0][0], met[turn][-1][0] + met[turn][-1][1]
        up = nn(vals_t[:, first:last], probs[first:last, cols[turn]])
        att[0, cols[turn], :] = up.T.astype(BF)
        if turn == 0:
            fine = nn(keys_t[:, : 3 * block], dscores[: 3 * block, cols[turn]])
        else:
            fine = nn(keys_t[:, block : 3 * block], dscores[block : 3 * block, cols[turn]])
            tail = columns - block
            fine = fine + nn(keys_t[:, tail:], dscores[tail:, cols[turn]])
        total_q[turn] = fine.T
        for level in range(1, LEVELS + 1):
            spots = [(s, z) for s, z, _, lev in segments if lev == level]
            start, size = spots[0][0], spots[0][1] + spots[1][1]
            up = nn(keys_t[:, start : start + size], dscores[start : start + size, cols[turn]])
            rows[turn, level - 1] = up.T
            factor = 2**level
            groups = block // factor
            mean = rows[turn, level - 1, pl.ds(0, groups, stride=factor), :]
            for row in range(1, factor):
                mean = mean + rows[turn, level - 1, pl.ds(row, groups, stride=factor), :]
            mean = mean * (1.0 / factor)
            for row in range(factor):
                spot = pl.ds(row, groups, stride=factor)
                total_q[turn, spot, :] = total_q[turn, spot, :] + mean
        gq[0, cols[turn], :] = (total_q[turn] * scale).astype(BF)

    places = [(g_out, None), (own, 0), (own, block)]
    for level in range(LEVELS):
        places += [(g_as[level], None), (g_bs[level], None)]
    places.append((g_in, None))
    for (ref, offset), (start, size, bias, level) in zip(places, segments):
        queries = pl.ds(0, 2 * block)
        if ref is g_out:
            queries = cols[0]
        if ref is g_in:
            queries = cols[1]
        right = rep_ref[level - 1, 0, queries, :] if level else q_ref[0, queries, :]
        here = pl.ds(start, size)
        gk = nn(dscores[here, queries], right) * scale
        gv = nn(probs[here, queries], d_ref[0, queries, :])
        for which, value in enumerate((gk, gv)):
            if offset is None:
                ref[which, 0] = value.astype(BF)
            else:
                ref[which, 0, pl.ds(offset, size), :] = value


def attend(place, count, q, d, rep, outer, inner, rim_out, rim_in, crossed_a, crossed_b):
    heads, block = inner.shape[1], inner.shape[2]
    span = 2 * block
    sizes = [span // 2 ** (level + 1) for level in range(LEVELS)]
    columns = 4 * block + 2 * sum(sizes)
    width = columns - block

    def pair(size):
        return pl.BlockSpec((2, 1, size, 128), lambda h: (0, h, 0, 0))

    head_spec = pl.BlockSpec((1, span, 128), lambda h: (h, 0, 0))
    flops = 2 * heads * span * width * 128 * 6
    return pl.pallas_call(
        functools.partial(attend_kernel, count),
        grid=(heads,),
        in_specs=[
            SMEM_SPEC,
            head_spec,
            head_spec,
            pl.BlockSpec((LEVELS, 1, span, 128), lambda h: (0, h, 0, 0)),
        ]
        + [pair(block)] * 4
        + [pair(size) for size in sizes] * 2,
        out_specs=[head_spec, head_spec, pair(span), pair(block), pair(block)]
        + [pair(size) for size in sizes] * 2,
        out_shape=[
            shape((heads, span, 128)),
            shape((heads, span, 128)),
            shape((2, heads, span, 128), F32),
            shape((2, heads, block, 128)),
            shape((2, heads, block, 128)),
        ]
        + [shape((2, heads, size, 128)) for size in sizes] * 2,
        scratch_shapes=[
            pltpu.VMEM((columns, 128), BF),
            pltpu.VMEM((columns, 128), BF),
            pltpu.VMEM((128, columns), BF),
            pltpu.VMEM((128, columns), BF),
            pltpu.VMEM((2, columns, block), F32),
            pltpu.VMEM((2, columns, block), F32),
            pltpu.VMEM((columns, span), BF),
            pltpu.VMEM((columns, span), BF),
            pltpu.VMEM((2, LEVELS, block, 128), F32),
            pltpu.VMEM((2, block, 128), F32),
        ],
        compiler_params=params(30),
        name="attend",
        cost_estimate=pl.CostEstimate(
            flops=flops, bytes_accessed=8 * 2**20, transcendentals=heads * span * width
        ),
    )(place, q, d, rep, outer, inner, rim_out, rim_in, *crossed_a, *crossed_b)


def join_kernel(heads, place_ref, att, gq, att_out, gq_out, wide):
    span = att.shape[1]
    odd = lax.rem(place_ref[0], 2)
    for ref, out in ((att, att_out), (gq, gq_out)):
        for head in range(heads):
            wide[pl.ds(head, span, stride=heads), :] = ref[head].astype(F32)
        turned_back(out, wide, odd)


def join(place, att, gq):
    heads, span = att.shape[:2]
    return pl.pallas_call(
        functools.partial(join_kernel, heads),
        out_shape=[shape((heads * span, 128))] * 2,
        in_specs=[SMEM_SPEC, VMEM_SPEC, VMEM_SPEC],
        scratch_shapes=[pltpu.VMEM((heads * span, 128), F32)],
        compiler_params=params(12),
        name="join",
        cost_estimate=pl.CostEstimate(flops=0, bytes_accessed=4 * 2**20, transcendentals=0),
    )(place, att, gq)


def gather_kernel(heads, place_ref, own, outer, inner, *refs):
    downs, ups, outs = refs[:LEVELS], refs[LEVELS : 2 * LEVELS], refs[2 * LEVELS : 2 * LEVELS + 2]
    wide, mine, spread = refs[2 * LEVELS + 2 :]
    span = own.shape[2]
    block = span // 2
    odd = lax.rem(place_ref[0], 2)
    for which, out in enumerate(outs):
        for head in range(heads):
            both = None
            for level in reversed(range(LEVELS)):
                value = downs[level][which, head].astype(F32) + ups[level][which, head].astype(F32)
                value = value * (1.0 / 2 ** (level + 1))
                if both is not None:
                    size = both.shape[0]
                    spread[pl.ds(0, size, stride=2), :] = both
                    spread[pl.ds(1, size, stride=2), :] = both
                    value = value + spread[pl.ds(0, 2 * size), :]
                both = value
            mine[pl.ds(0, block), :] = own[which, head, :block] + outer[which, head].astype(F32)
            mine[pl.ds(block, block), :] = own[which, head, block:] + inner[which, head].astype(F32)
            for second in range(2):
                wide[pl.ds(head + heads * second, block, stride=2 * heads), :] = (
                    mine[pl.ds(second, block, stride=2), :] + both
                )
        turned_back(out, wide, odd)


def gather(place, own, *sums):
    heads, span = own.shape[1:3]
    return pl.pallas_call(
        functools.partial(gather_kernel, heads),
        out_shape=[shape((heads * span, 128))] * 2,
        in_specs=[SMEM_SPEC] + [VMEM_SPEC] * (1 + len(sums)),
        scratch_shapes=[
            pltpu.VMEM((heads * span, 128), F32),
            pltpu.VMEM((span, 128), F32),
            pltpu.VMEM((span // 2, 128), F32),
        ],
        compiler_params=params(16),
        name="gather",
        cost_estimate=pl.CostEstimate(flops=0, bytes_accessed=8 * 2**20, transcendentals=0),
    )(place, own, *sums)


def local(query, key, value, dout):
    span, heads, width = query.shape
    count = lax.axis_size("seq")
    place = jnp.reshape(lax.axis_index("seq"), (1,)).astype(jnp.int32)
    flat = (heads * span, width)
    q2, k2, v2, d2 = (x.reshape(flat) for x in (query, key, value, dout))
    outer, inner, *coarse = split_kv(place, k2, v2, heads, span)
    crossed_b, crossed_a, rims = exchange(coarse, coarse, outer, inner)
    qh, dh, rep = split_qd(place, q2, d2, heads, span)
    att, gq, own, g_out, g_in, *grads = attend(
        place, count, qh, dh, rep, outer, inner, *rims, crossed_a, crossed_b
    )
    downs, ups, rims = exchange(grads[:LEVELS], grads[LEVELS:], g_out, g_in)
    attended, grad_query = join(place, att, gq)
    grad_key, grad_value = gather(place, own, *rims, *downs, *ups)
    return tuple(
        x.reshape(span, heads, width) for x in (attended, grad_query, grad_key, grad_value)
    )


def solution(mesh):
    placed = P("seq", "head", None)
    return jax.shard_map(
        local,
        mesh=mesh,
        in_specs=(placed,) * 4,
        out_specs=(placed,) * 4,
        check_vma=False,
    )
```

```python
import functools
import math

import jax
import jax.numpy as jnp
from jax import lax
from jax.experimental import pallas as pl
from jax.experimental.pallas import tpu as pltpu
from jax.sharding import PartitionSpec as P

BLOCK = 256
LEVELS = 3
CHUNKS = 2
LOG2E = math.log2(math.e)

BF = jnp.bfloat16
F32 = jnp.float32


def crossed(value, steps):
    count = lax.axis_size("seq")
    pairs = [(at, at + (steps if at % 2 == 0 else -steps)) for at in range(count)]
    return lax.ppermute(value, "seq", [(at, to) for at, to in pairs if 0 <= to < count])


def swapped(value, across):
    count = lax.axis_size("seq")
    pairs = [(at, at ^ 1) for at in range(count)]
    if across:
        pairs = [(at, at + 1 if at % 2 else at - 1) for at in range(count)]
    return lax.ppermute(value, "seq", [(at, to) for at, to in pairs if 0 <= to < count])


def nt(left, right):
    return lax.dot_general(left, right, (((1,), (1,)), ((), ())), preferred_element_type=F32)


def nn(left, right):
    return jnp.dot(left, right, preferred_element_type=F32)


def shape(dims, dtype=BF):
    return jax.ShapeDtypeStruct(dims, dtype)


def params(mib):
    return pltpu.CompilerParams(vmem_limit_bytes=mib * 2**20)


SMEM_SPEC = pl.BlockSpec(memory_space=pltpu.SMEM)
VMEM_SPEC = pl.BlockSpec(memory_space=pltpu.VMEM)


def turned(wide, ref, odd):
    half = wide.shape[0] // 2
    wide[pl.ds(pl.multiple_of(odd * half, half), half), :] = ref[:half].astype(F32)
    wide[pl.ds(pl.multiple_of((1 - odd) * half, half), half), :] = ref[half:].astype(F32)


def turned_back(ref, wide, odd):
    half = wide.shape[0] // 2
    ref[pl.ds(pl.multiple_of(odd * half, half), half), :] = wide[:half].astype(BF)
    ref[pl.ds(pl.multiple_of((1 - odd) * half, half), half), :] = wide[half:].astype(BF)


def pair_sums(wide, row, size, heads):
    return (
        wide[pl.ds(row, size, stride=2 * heads), :]
        + wide[pl.ds(row + heads, size, stride=2 * heads), :]
    )


def next_sums(sums, total):
    size = total.shape[0]
    sums[pl.ds(0, size), :] = total
    half = size // 2
    return sums[pl.ds(0, half, stride=2), :] + sums[pl.ds(1, half, stride=2), :]


def split_kv_kernel(heads, place_ref, k_ref, v_ref, outer, inner, *rest):
    coarse, (wide, sums) = rest[:LEVELS], rest[LEVELS:]
    block = inner.shape[2]
    odd = lax.rem(place_ref[0], 2)
    for at, ref in enumerate((k_ref, v_ref)):
        turned(wide, ref, odd)
        for head in range(heads):
            outer[at, head] = wide[pl.ds(head, block, stride=heads), :].astype(BF)
            inner[at, head] = wide[pl.ds(head + heads * block, block, stride=heads), :].astype(BF)
            total = pair_sums(wide, head, block, heads)
            for level in range(LEVELS):
                coarse[level][at, head] = (total * (1.0 / 2 ** (level + 1))).astype(BF)
                if level + 1 < LEVELS:
                    total = next_sums(sums, total)


def split_kv(place, k2, v2, heads, span):
    block = span // 2
    outs = [shape((2, heads, block, 128))] * 2
    outs += [shape((2, heads, span // 2 ** (level + 1), 128)) for level in range(LEVELS)]
    return pl.pallas_call(
        functools.partial(split_kv_kernel, heads),
        out_shape=outs,
        in_specs=[SMEM_SPEC, VMEM_SPEC, VMEM_SPEC],
        scratch_shapes=[
            pltpu.VMEM((heads * span, 128), F32),
            pltpu.VMEM((block, 128), F32),
        ],
        compiler_params=params(16),
        name="split_kv",
        cost_estimate=pl.CostEstimate(flops=0, bytes_accessed=4 * 2**20, transcendentals=0),
    )(place, k2, v2)


def later_kernel(count, *refs):
    outs = refs[len(refs) - count * CHUNKS :]
    for at in range(count):
        per = refs[at].shape[1] // CHUNKS
        for chunk in range(CHUNKS):
            outs[chunk * count + at][...] = refs[at][:, chunk * per : (chunk + 1) * per]


def later(after, arrays):
    halves = [shape((2, x.shape[1] // CHUNKS, *x.shape[2:])) for x in arrays]
    outs = pl.pallas_call(
        functools.partial(later_kernel, len(arrays)),
        out_shape=halves * CHUNKS,
        in_specs=[VMEM_SPEC] * len(arrays) + [pl.BlockSpec(memory_space=pl.ANY)] * len(after),
        compiler_params=params(8),
        name="later",
        cost_estimate=pl.CostEstimate(flops=0, bytes_accessed=2 * 2**20, transcendentals=0),
    )(*arrays, *after)
    count = len(arrays)
    return [outs[chunk * count : (chunk + 1) * count] for chunk in range(CHUNKS)]


def split_qd_kernel(heads, place_ref, q_ref, d_ref, q_out, d_out, rep_out, wide, sums, spread):
    span = q_out.shape[1]
    odd = lax.rem(place_ref[0], 2)
    turned(wide, d_ref, odd)
    for head in range(heads):
        d_out[head] = wide[pl.ds(head, span, stride=heads), :].astype(BF)
    turned(wide, q_ref, odd)
    for head in range(heads):
        q_out[head] = wide[pl.ds(head, span, stride=heads), :].astype(BF)
        total = pair_sums(wide, head, span // 2, heads)
        for level in range(LEVELS):
            factor = 2 ** (level + 1)
            mean = (total * (1.0 / factor)).astype(BF).astype(F32)
            for row in range(factor):
                spread[pl.ds(row, span // factor, stride=factor), :] = mean
            rep_out[level, head] = spread[...].astype(BF)
            if level + 1 < LEVELS:
                total = next_sums(sums, total)


def split_qd(place, q2, d2, heads, span):
    return pl.pallas_call(
        functools.partial(split_qd_kernel, heads),
        out_shape=[
            shape((heads, span, 128)),
            shape((heads, span, 128)),
            shape((LEVELS, heads, span, 128)),
        ],
        in_specs=[SMEM_SPEC] + [VMEM_SPEC] * 2,
        scratch_shapes=[
            pltpu.VMEM((heads * span, 128), F32),
            pltpu.VMEM((span // 2, 128), F32),
            pltpu.VMEM((span, 128), F32),
        ],
        compiler_params=params(16),
        name="split_qd",
        cost_estimate=pl.CostEstimate(flops=0, bytes_accessed=8 * 2**20, transcendentals=0),
    )(place, q2, d2)


def attend_kernel(
    count, skip, place_ref, q_ref, d_ref, rep_ref, outer, inner, rim_out, rim_in, *rest
):
    crossed_a, crossed_b = rest[:LEVELS], rest[LEVELS : 2 * LEVELS]
    rest = rest[: 2 * LEVELS] + rest[2 * LEVELS + skip :]
    att, gq, own, g_out, g_in = rest[2 * LEVELS : 2 * LEVELS + 5]
    rest = rest[2 * LEVELS + 5 :]
    g_as, g_bs = rest[:LEVELS], rest[LEVELS : 2 * LEVELS]
    keys, vals, keys_t, vals_t, scores, grads, probs, dscores, rows, total_q = rest[2 * LEVELS :]
    place = place_ref[0]
    even = lax.rem(place, 2) == 0
    block = outer.shape[2]
    scale = 1.0 / math.sqrt(128)
    scale2 = scale * LOG2E

    def reaches(below, steps):
        return jnp.where(below, place >= steps, place < count - steps)

    parts = [(rim_out, reaches(even, 1), 0), (outer, None, 0), (inner, None, 0)]
    for level in range(LEVELS):
        factor = 2 ** (level + 1)
        parts.append((crossed_a[level], reaches(even, factor), level + 1))
        parts.append((crossed_b[level], reaches(jnp.logical_not(even), factor), level + 1))
    parts.append((rim_in, None, 0))
    at = 0
    segments = []
    for ref, ok, level in parts:
        size = ref.shape[2]
        keys[pl.ds(at, size), :] = ref[0, 0]
        vals[pl.ds(at, size), :] = ref[1, 0]
        bias = float(level)
        if ok is not None:
            bias = jnp.where(ok, bias, -jnp.inf).astype(F32)
        segments.append((at, size, bias, level))
        at += size
    columns = at
    keys_t[...] = keys[...].T
    vals_t[...] = vals[...].T

    turns = (0, 1)
    cols = [pl.ds(turn * block, block) for turn in turns]
    met = [segments[:-1], segments[1:]]
    top = [None, None]
    for turn in turns:
        d_blk = d_ref[0, cols[turn], :]
        using = [q_ref[0, cols[turn], :]]
        using += [rep_ref[level, 0, cols[turn], :] for level in range(LEVELS)]
        for start, size, bias, level in met[turn]:
            here = pl.ds(start, size)
            s = nt(keys[here, :], using[level])
            scores[turn, here, :] = s
            high = jnp.max(s, axis=0, keepdims=True) * scale2 + bias
            top[turn] = high if top[turn] is None else jnp.maximum(top[turn], high)
            grads[turn, here, :] = nt(vals[here, :], d_blk)
    inverse, delta = [None, None], [None, None]
    for turn in turns:
        total = jnp.zeros((1, block), F32)
        acc = jnp.zeros((1, block), F32)
        for start, size, bias, level in met[turn]:
            here = pl.ds(start, size)
            e = jnp.exp2(scores[turn, here, :] * scale2 - (top[turn] - bias))
            scores[turn, here, :] = e
            total = total + jnp.sum(e, axis=0, keepdims=True)
            acc = acc + jnp.sum(e * grads[turn, here, :], axis=0, keepdims=True)
        inverse[turn] = 1.0 / total
        delta[turn] = acc * inverse[turn]
    for turn in turns:
        for start, size, bias, level in met[turn]:
            here = pl.ds(start, size)
            p = scores[turn, here, :] * inverse[turn]
            probs[here, cols[turn]] = p.astype(BF)
            dscores[here, cols[turn]] = (p * (grads[turn, here, :] - delta[turn])).astype(BF)
        first, last = met[turn][0][0], met[turn][-1][0] + met[turn][-1][1]
        up = nn(vals_t[:, first:last], probs[first:last, cols[turn]])
        att[0, cols[turn], :] = up.T.astype(BF)
        if turn == 0:
            fine = nn(keys_t[:, : 3 * block], dscores[: 3 * block, cols[turn]])
        else:
            fine = nn(keys_t[:, block : 3 * block], dscores[block : 3 * block, cols[turn]])
            tail = columns - block
            fine = fine + nn(keys_t[:, tail:], dscores[tail:, cols[turn]])
        total_q[turn] = fine.T
        for level in range(1, LEVELS + 1):
            spots = [(s, z) for s, z, _, lev in segments if lev == level]
            start, size = spots[0][0], spots[0][1] + spots[1][1]
            up = nn(keys_t[:, start : start + size], dscores[start : start + size, cols[turn]])
            rows[turn, level - 1] = up.T
            factor = 2**level
            groups = block // factor
            mean = rows[turn, level - 1, pl.ds(0, groups, stride=factor), :]
            for row in range(1, factor):
                mean = mean + rows[turn, level - 1, pl.ds(row, groups, stride=factor), :]
            mean = mean * (1.0 / factor)
            for row in range(factor):
                spot = pl.ds(row, groups, stride=factor)
                total_q[turn, spot, :] = total_q[turn, spot, :] + mean
        gq[0, cols[turn], :] = (total_q[turn] * scale).astype(BF)

    places = [(g_out, None), (own, 0), (own, block)]
    for level in range(LEVELS):
        places += [(g_as[level], None), (g_bs[level], None)]
    places.append((g_in, None))
    for (ref, offset), (start, size, bias, level) in zip(places, segments):
        queries = pl.ds(0, 2 * block)
        if ref is g_out:
            queries = cols[0]
        if ref is g_in:
            queries = cols[1]
        right = rep_ref[level - 1, 0, queries, :] if level else q_ref[0, queries, :]
        here = pl.ds(start, size)
        gk = nn(dscores[here, queries], right) * scale
        gv = nn(probs[here, queries], d_ref[0, queries, :])
        for which, value in enumerate((gk, gv)):
            if offset is None:
                ref[which, 0] = value.astype(BF)
            else:
                ref[which, 0, pl.ds(offset, size), :] = value


def attend(chunk, before, place, count, q, d, rep, outer, inner, rims, crossed_a, crossed_b):
    heads, block = inner.shape[1], inner.shape[2]
    per = heads // CHUNKS
    base = chunk * per
    span = 2 * block
    sizes = [span // 2 ** (level + 1) for level in range(LEVELS)]
    columns = 4 * block + 2 * sum(sizes)
    width = columns - block

    def pair(size, first=base):
        return pl.BlockSpec((2, 1, size, 128), lambda h: (0, first + h, 0, 0))

    head_spec = pl.BlockSpec((1, span, 128), lambda h: (base + h, 0, 0))
    flops = 2 * per * span * width * 128 * 6
    in_specs = [
        SMEM_SPEC,
        head_spec,
        head_spec,
        pl.BlockSpec((LEVELS, 1, span, 128), lambda h: (0, base + h, 0, 0)),
    ]
    in_specs += [pair(block)] * 4
    in_specs += [pair(size, 0) for size in sizes] + [pair(size) for size in sizes]
    aliases = {len(in_specs) + at: at for at in range(len(before))}
    return pl.pallas_call(
        functools.partial(attend_kernel, count, len(before)),
        grid=(per,),
        in_specs=in_specs + [pl.BlockSpec(memory_space=pl.ANY)] * len(before),
        out_specs=[head_spec, head_spec, pair(span), pair(block), pair(block)]
        + [pair(size) for size in sizes] * 2,
        out_shape=[
            shape((heads, span, 128)),
            shape((heads, span, 128)),
            shape((2, heads, span, 128), F32),
            shape((2, heads, block, 128)),
            shape((2, heads, block, 128)),
        ]
        + [shape((2, heads, size, 128)) for size in sizes] * 2,
        scratch_shapes=[
            pltpu.VMEM((columns, 128), BF),
            pltpu.VMEM((columns, 128), BF),
            pltpu.VMEM((128, columns), BF),
            pltpu.VMEM((128, columns), BF),
            pltpu.VMEM((2, columns, block), F32),
            pltpu.VMEM((2, columns, block), F32),
            pltpu.VMEM((columns, span), BF),
            pltpu.VMEM((columns, span), BF),
            pltpu.VMEM((2, LEVELS, block, 128), F32),
            pltpu.VMEM((2, block, 128), F32),
        ],
        input_output_aliases=aliases,
        compiler_params=params(30),
        name="attend",
        cost_estimate=pl.CostEstimate(
            flops=flops, bytes_accessed=8 * 2**20, transcendentals=per * span * width
        ),
    )(place, q, d, rep, outer, inner, *rims, *crossed_a, *crossed_b, *before)


def merge_kernel(count, coarse, fine, *refs):
    outs, wide = refs[len(refs) - count - 2 : -1], refs[-1]
    rows = fine.shape[0]
    half = coarse[...].astype(F32) * 0.5
    wide[pl.ds(0, rows // 2, stride=2), :] = half
    wide[pl.ds(1, rows // 2, stride=2), :] = half
    outs[0][...] = (wide[...] + fine[...].astype(F32)).astype(BF)
    for at in range(count):
        outs[1 + at][...] = refs[at][...]


def merge(coarse, fine, rest=(), after=()):
    flat = [x.reshape(-1, 128) for x in (coarse, fine, *rest)]
    outs = pl.pallas_call(
        functools.partial(merge_kernel, len(rest)),
        out_shape=[shape(x.shape) for x in flat[1:]],
        in_specs=[VMEM_SPEC] * len(flat) + [pl.BlockSpec(memory_space=pl.ANY)] * len(after),
        scratch_shapes=[pltpu.VMEM(flat[1].shape, F32)],
        compiler_params=params(12),
        name="merge",
        cost_estimate=pl.CostEstimate(flops=0, bytes_accessed=2 * 2**20, transcendentals=0),
    )(*flat, *after)
    return [x.reshape(y.shape) for x, y in zip(outs, (fine, *rest))]


def join_kernel(heads, place_ref, att, gq, att_out, gq_out, wide):
    span = att.shape[1]
    odd = lax.rem(place_ref[0], 2)
    for ref, out in ((att, att_out), (gq, gq_out)):
        for head in range(heads):
            wide[pl.ds(head, span, stride=heads), :] = ref[head].astype(F32)
        turned_back(out, wide, odd)


def join(place, att, gq):
    heads, span = att.shape[:2]
    return pl.pallas_call(
        functools.partial(join_kernel, heads),
        out_shape=[shape((heads * span, 128))] * 2,
        in_specs=[SMEM_SPEC, VMEM_SPEC, VMEM_SPEC],
        scratch_shapes=[pltpu.VMEM((heads * span, 128), F32)],
        compiler_params=params(12),
        name="join",
        cost_estimate=pl.CostEstimate(flops=0, bytes_accessed=4 * 2**20, transcendentals=0),
    )(place, att, gq)


def gather_kernel(heads, place_ref, own, outer, inner, *refs):
    downs, ups, outs, (wide, mine, spread) = refs[:2], refs[2:4], refs[4:6], refs[6:]
    span = own.shape[2]
    block = span // 2
    odd = lax.rem(place_ref[0], 2)
    for which, out in enumerate(outs):
        for head in range(heads):
            both = None
            for level in (1, 0):
                value = downs[level][which, head].astype(F32) + ups[level][which, head].astype(F32)
                value = value * (1.0 / 2 ** (level + 1))
                if both is not None:
                    size = both.shape[0]
                    spread[pl.ds(0, size, stride=2), :] = both
                    spread[pl.ds(1, size, stride=2), :] = both
                    value = value + spread[pl.ds(0, 2 * size), :]
                both = value
            mine[pl.ds(0, block), :] = own[which, head, :block] + outer[which, head].astype(F32)
            mine[pl.ds(block, block), :] = own[which, head, block:] + inner[which, head].astype(F32)
            for second in range(2):
                wide[pl.ds(head + heads * second, block, stride=2 * heads), :] = (
                    mine[pl.ds(second, block, stride=2), :] + both
                )
        turned_back(out, wide, odd)


def gather(place, own, *sums):
    heads, span = own.shape[1:3]
    return pl.pallas_call(
        functools.partial(gather_kernel, heads),
        out_shape=[shape((heads * span, 128))] * 2,
        in_specs=[SMEM_SPEC] + [VMEM_SPEC] * (1 + len(sums)),
        scratch_shapes=[
            pltpu.VMEM((heads * span, 128), F32),
            pltpu.VMEM((span, 128), F32),
            pltpu.VMEM((span // 2, 128), F32),
        ],
        compiler_params=params(16),
        name="gather",
        cost_estimate=pl.CostEstimate(flops=0, bytes_accessed=8 * 2**20, transcendentals=0),
    )(place, own, *sums)


def local(query, key, value, dout):
    span, heads, width = query.shape
    count = lax.axis_size("seq")
    place = jnp.reshape(lax.axis_index("seq"), (1,)).astype(jnp.int32)
    flat = (heads * span, width)
    q2, k2, v2, d2 = (x.reshape(flat) for x in (query, key, value, dout))
    outer, inner, *coarse = split_kv(place, k2, v2, heads, span)
    steps = [2 ** (level + 1) for level in range(LEVELS)]
    crossed_b = [crossed(x, -step) for x, step in zip(coarse, steps)]
    rims = swapped(outer, True), swapped(inner, False)
    chunks = later((*crossed_b[1:], rims[1]), coarse)
    qh, dh, rep = split_qd(place, q2, d2, heads, span)
    results = ()
    for chunk in range(CHUNKS):
        crossed_a = [crossed(x, step) for x, step in zip(chunks[chunk], steps)]
        results = attend(
            chunk, results, place, count, qh, dh, rep, outer, inner, rims, crossed_a, crossed_b
        )
    att, gq, own, g_out, g_in, *grads = results
    g_as, g_bs = grads[:LEVELS], grads[LEVELS:]
    far_a, one_a = crossed(g_as[2], -4), crossed(g_as[0], -2)
    g_out, g_in = swapped(g_out, True), swapped(g_in, False)
    mid_a, far_b, one_b = merge(far_a, g_as[1], (g_bs[2], g_bs[0]), (g_in,))
    far_b, one_b, two_a = crossed(far_b, 4), crossed(one_b, 2), crossed(mid_a, -4)
    two_b = crossed(merge(far_b, g_bs[1])[0], 4)
    attended, grad_query = join(place, att, gq)
    grad_key, grad_value = gather(place, own, g_out, g_in, one_a, two_a, one_b, two_b)
    return tuple(
        x.reshape(span, heads, width) for x in (attended, grad_query, grad_key, grad_value)
    )


def solution(mesh):
    placed = P("seq", "head", None)
    return jax.shard_map(
        local,
        mesh=mesh,
        in_specs=(placed,) * 4,
        out_specs=(placed,) * 4,
        check_vma=False,
    )
```

```python
import functools
import math

import jax
import jax.numpy as jnp
from jax import lax
from jax.experimental import pallas as pl
from jax.experimental.pallas import tpu as pltpu
from jax.sharding import PartitionSpec as P

BLOCK = 256
LEVELS = 3
LOG2E = math.log2(math.e)

BF = jnp.bfloat16
F32 = jnp.float32


def crossed(value, steps):
    count = lax.axis_size("seq")
    pairs = [(at, at + (steps if at % 2 == 0 else -steps)) for at in range(count)]
    return lax.ppermute(value, "seq", [(at, to) for at, to in pairs if 0 <= to < count])


def swapped(value, across):
    count = lax.axis_size("seq")
    pairs = [(at, at ^ 1) for at in range(count)]
    if across:
        pairs = [(at, at + 1 if at % 2 else at - 1) for at in range(count)]
    return lax.ppermute(value, "seq", [(at, to) for at, to in pairs if 0 <= to < count])


def nt(left, right):
    return lax.dot_general(left, right, (((1,), (1,)), ((), ())), preferred_element_type=F32)


def nn(left, right):
    return jnp.dot(left, right, preferred_element_type=F32)


def shape(dims, dtype=BF):
    return jax.ShapeDtypeStruct(dims, dtype)


def params(mib):
    return pltpu.CompilerParams(vmem_limit_bytes=mib * 2**20)


SMEM_SPEC = pl.BlockSpec(memory_space=pltpu.SMEM)
VMEM_SPEC = pl.BlockSpec(memory_space=pltpu.VMEM)


def turned(wide, ref, odd):
    half = wide.shape[0] // 2
    wide[pl.ds(pl.multiple_of(odd * half, half), half), :] = ref[:half].astype(F32)
    wide[pl.ds(pl.multiple_of((1 - odd) * half, half), half), :] = ref[half:].astype(F32)


def turned_back(ref, wide, odd):
    half = wide.shape[0] // 2
    ref[pl.ds(pl.multiple_of(odd * half, half), half), :] = wide[:half].astype(BF)
    ref[pl.ds(pl.multiple_of((1 - odd) * half, half), half), :] = wide[half:].astype(BF)


def pair_sums(wide, row, size, heads):
    return (
        wide[pl.ds(row, size, stride=2 * heads), :]
        + wide[pl.ds(row + heads, size, stride=2 * heads), :]
    )


def next_sums(sums, total):
    size = total.shape[0]
    sums[pl.ds(0, size), :] = total
    half = size // 2
    return sums[pl.ds(0, half, stride=2), :] + sums[pl.ds(1, half, stride=2), :]


def split_kv_kernel(heads, place_ref, k_ref, v_ref, outer, inner, *rest):
    coarse, (wide, sums) = rest[:LEVELS], rest[LEVELS:]
    block = inner.shape[2]
    odd = lax.rem(place_ref[0], 2)
    for at, ref in enumerate((k_ref, v_ref)):
        turned(wide, ref, odd)
        for head in range(heads):
            outer[at, head] = wide[pl.ds(head, block, stride=heads), :].astype(BF)
            inner[at, head] = wide[pl.ds(head + heads * block, block, stride=heads), :].astype(BF)
            total = pair_sums(wide, head, block, heads)
            for level in range(LEVELS):
                coarse[level][at, head] = (total * (1.0 / 2 ** (level + 1))).astype(BF)
                if level + 1 < LEVELS:
                    total = next_sums(sums, total)


def split_kv(place, k2, v2, heads, span):
    block = span // 2
    outs = [shape((2, heads, block, 128))] * 2
    outs += [shape((2, heads, span // 2 ** (level + 1), 128)) for level in range(LEVELS)]
    return pl.pallas_call(
        functools.partial(split_kv_kernel, heads),
        out_shape=outs,
        in_specs=[SMEM_SPEC, VMEM_SPEC, VMEM_SPEC],
        scratch_shapes=[
            pltpu.VMEM((heads * span, 128), F32),
            pltpu.VMEM((block, 128), F32),
        ],
        compiler_params=params(16),
        name="split_kv",
        cost_estimate=pl.CostEstimate(flops=0, bytes_accessed=4 * 2**20, transcendentals=0),
    )(place, k2, v2)


def later_kernel(count, *refs):
    for at in range(count):
        refs[len(refs) - count + at][...] = refs[at][...]


def later(after, arrays):
    return pl.pallas_call(
        functools.partial(later_kernel, len(arrays)),
        out_shape=[shape(x.shape) for x in arrays],
        in_specs=[VMEM_SPEC] * len(arrays) + [pl.BlockSpec(memory_space=pl.ANY)] * len(after),
        compiler_params=params(8),
        name="later",
        cost_estimate=pl.CostEstimate(flops=0, bytes_accessed=2 * 2**20, transcendentals=0),
    )(*arrays, *after)


def exchange(firsts, seconds, outer, inner):
    steps = [2 ** (level + 1) for level in range(LEVELS)]
    down = [crossed(x, -step) for x, step in zip(firsts, steps)]
    rims = swapped(outer, True), swapped(inner, False)
    up = [
        crossed(x, step) for x, step in zip(later((*down[1:], rims[1]), seconds), steps)
    ]
    return down, up, rims


def split_qd_kernel(heads, place_ref, q_ref, d_ref, q_out, d_out, rep_out, wide, sums, spread):
    span = q_out.shape[1]
    odd = lax.rem(place_ref[0], 2)
    turned(wide, d_ref, odd)
    for head in range(heads):
        d_out[head] = wide[pl.ds(head, span, stride=heads), :].astype(BF)
    turned(wide, q_ref, odd)
    for head in range(heads):
        q_out[head] = wide[pl.ds(head, span, stride=heads), :].astype(BF)
        total = pair_sums(wide, head, span // 2, heads)
        for level in range(LEVELS):
            factor = 2 ** (level + 1)
            mean = (total * (1.0 / factor)).astype(BF).astype(F32)
            for row in range(factor):
                spread[pl.ds(row, span // factor, stride=factor), :] = mean
            rep_out[level, head] = spread[...].astype(BF)
            if level + 1 < LEVELS:
                total = next_sums(sums, total)


def split_qd(place, q2, d2, heads, span):
    return pl.pallas_call(
        functools.partial(split_qd_kernel, heads),
        out_shape=[
            shape((heads, span, 128)),
            shape((heads, span, 128)),
            shape((LEVELS, heads, span, 128)),
        ],
        in_specs=[SMEM_SPEC] + [VMEM_SPEC] * 2,
        scratch_shapes=[
            pltpu.VMEM((heads * span, 128), F32),
            pltpu.VMEM((span // 2, 128), F32),
            pltpu.VMEM((span, 128), F32),
        ],
        compiler_params=params(16),
        name="split_qd",
        cost_estimate=pl.CostEstimate(flops=0, bytes_accessed=8 * 2**20, transcendentals=0),
    )(place, q2, d2)


def attend_kernel(count, place_ref, q_ref, d_ref, rep_ref, outer, inner, rim_out, rim_in, *rest):
    crossed_a, crossed_b = rest[:LEVELS], rest[LEVELS : 2 * LEVELS]
    g_out, g_in = rest[2 * LEVELS : 2 * LEVELS + 2]
    rest = rest[2 * LEVELS + 2 :]
    g_as, g_bs = rest[:LEVELS], rest[LEVELS : 2 * LEVELS]
    probs, dscores, keys_t, vals_t, keys, vals, scores, grads = rest[2 * LEVELS :]
    place = place_ref[0]
    even = lax.rem(place, 2) == 0
    block = outer.shape[2]
    scale = 1.0 / math.sqrt(128)
    scale2 = scale * LOG2E

    def reaches(below, steps):
        return jnp.where(below, place >= steps, place < count - steps)

    parts = [(rim_out, reaches(even, 1), 0), (outer, None, 0), (inner, None, 0)]
    for level in range(LEVELS):
        factor = 2 ** (level + 1)
        parts.append((crossed_a[level], reaches(even, factor), level + 1))
        parts.append((crossed_b[level], reaches(jnp.logical_not(even), factor), level + 1))
    parts.append((rim_in, None, 0))
    at = 0
    segments = []
    for ref, ok, level in parts:
        size = ref.shape[2]
        keys[pl.ds(at, size), :] = ref[0, 0]
        vals[pl.ds(at, size), :] = ref[1, 0]
        bias = float(level)
        if ok is not None:
            bias = jnp.where(ok, bias, -jnp.inf).astype(F32)
        segments.append((at, size, bias, level))
        at += size
    keys_t[0] = keys[...].T
    vals_t[0] = vals[...].T

    turns = (0, 1)
    cols = [pl.ds(turn * block, block) for turn in turns]
    met = [segments[:-1], segments[1:]]
    d_blks = [d_ref[0, cols[turn], :] for turn in turns]
    using = [[q_ref[0, cols[turn], :]] for turn in turns]
    for turn in turns:
        using[turn] += [rep_ref[level, 0, cols[turn], :] for level in range(LEVELS)]
    top = [None, None]
    total = [jnp.zeros((1, block), F32)] * 2
    acc = [jnp.zeros((1, block), F32)] * 2

    def products(turn, start, size, bias, level):
        here = pl.ds(start, size)
        s = nt(keys[here, :], using[turn][level])
        scores[turn, here, :] = s
        high = jnp.max(s, axis=0, keepdims=True) * scale2 + bias
        top[turn] = high if top[turn] is None else jnp.maximum(top[turn], high)
        grads[turn, here, :] = nt(vals[here, :], d_blks[turn])

    def weights(turn, start, size, bias, level):
        here = pl.ds(start, size)
        e = jnp.exp2(scores[turn, here, :] * scale2 - (top[turn] - bias))
        scores[turn, here, :] = e
        total[turn] = total[turn] + jnp.sum(e, axis=0, keepdims=True)
        acc[turn] = acc[turn] + jnp.sum(e * grads[turn, here, :], axis=0, keepdims=True)

    for part in met[0]:
        products(0, *part)
    for part, other in zip(met[0], met[1]):
        products(1, *other)
        weights(0, *part)
    for part in met[1]:
        weights(1, *part)
    for turn in turns:
        inverse = 1.0 / total[turn]
        delta = acc[turn] * inverse
        for start, size, bias, level in met[turn]:
            here = pl.ds(start, size)
            p = scores[turn, here, :] * inverse
            probs[0, here, cols[turn]] = p.astype(BF)
            dscores[0, here, cols[turn]] = (p * (grads[turn, here, :] - delta)).astype(BF)

    places = [g_out, None, None]
    for level in range(LEVELS):
        places += [g_as[level], g_bs[level]]
    places.append(g_in)
    for ref, (start, size, bias, level) in zip(places, segments):
        if ref is None:
            continue
        queries = pl.ds(0, 2 * block)
        if ref is g_out:
            queries = cols[0]
        if ref is g_in:
            queries = cols[1]
        right = rep_ref[level - 1, 0, queries, :] if level else q_ref[0, queries, :]
        here = pl.ds(start, size)
        ref[0, 0] = (nn(dscores[0, here, queries], right) * scale).astype(BF)
        ref[1, 0] = nn(probs[0, here, queries], d_ref[0, queries, :]).astype(BF)


def finish_kernel(q_ref, d_ref, probs, dscores, keys_t, vals_t, att, gq, own, rows, total_q):
    span = q_ref.shape[1]
    block = span // 2
    columns = probs.shape[1]
    width = columns - block
    scale = 1.0 / math.sqrt(128)
    mine = pl.ds(block, span)
    own[0, 0] = nn(dscores[0, mine, :], q_ref[0]) * scale
    own[1, 0] = nn(probs[0, mine, :], d_ref[0])
    for turn in (0, 1):
        cols = pl.ds(turn * block, block)
        met = pl.ds(turn * block, width)
        att[0, cols, :] = nn(vals_t[0, :, met], probs[0, met, cols]).T.astype(BF)
        if turn == 0:
            fine = nn(keys_t[0, :, : 3 * block], dscores[0, : 3 * block, cols])
        else:
            fine = nn(keys_t[0, :, block : 3 * block], dscores[0, block : 3 * block, cols])
            fine = fine + nn(keys_t[0, :, width:], dscores[0, width:, cols])
        total_q[turn] = fine.T
        start = 3 * block
        for level in range(1, LEVELS + 1):
            size = 2 * (span // 2**level)
            here = pl.ds(start, size)
            start += size
            rows[turn, level - 1] = nn(keys_t[0, :, here], dscores[0, here, cols]).T
            factor = 2**level
            groups = block // factor
            mean = rows[turn, level - 1, pl.ds(0, groups, stride=factor), :]
            for row in range(1, factor):
                mean = mean + rows[turn, level - 1, pl.ds(row, groups, stride=factor), :]
            mean = mean * (1.0 / factor)
            for row in range(factor):
                spot = pl.ds(row, groups, stride=factor)
                total_q[turn, spot, :] = total_q[turn, spot, :] + mean
        gq[0, cols, :] = (total_q[turn] * scale).astype(BF)


def attend(place, count, q, d, rep, outer, inner, rim_out, rim_in, crossed_a, crossed_b):
    heads, block = inner.shape[1], inner.shape[2]
    span = 2 * block
    sizes = [span // 2 ** (level + 1) for level in range(LEVELS)]
    columns = 4 * block + 2 * sum(sizes)
    width = columns - block

    def pair(size):
        return pl.BlockSpec((2, 1, size, 128), lambda h: (0, h, 0, 0))

    head_spec = pl.BlockSpec((1, span, 128), lambda h: (h, 0, 0))
    flops = 2 * heads * span * width * 128 * 6
    return pl.pallas_call(
        functools.partial(attend_kernel, count),
        grid=(heads,),
        in_specs=[
            SMEM_SPEC,
            head_spec,
            head_spec,
            pl.BlockSpec((LEVELS, 1, span, 128), lambda h: (0, h, 0, 0)),
        ]
        + [pair(block)] * 4
        + [pair(size) for size in sizes] * 2,
        out_specs=[pair(size) for size in [block, block] + sizes * 2]
        + [pl.BlockSpec((1, columns, span), lambda h: (h, 0, 0))] * 2
        + [pl.BlockSpec((1, 128, columns), lambda h: (h, 0, 0))] * 2,
        out_shape=[shape((2, heads, size, 128)) for size in [block, block] + sizes * 2]
        + [shape((heads, columns, span))] * 2
        + [shape((heads, 128, columns))] * 2,
        scratch_shapes=[
            pltpu.VMEM((columns, 128), BF),
            pltpu.VMEM((columns, 128), BF),
            pltpu.VMEM((2, columns, block), F32),
            pltpu.VMEM((2, columns, block), F32),
        ],
        compiler_params=params(30),
        name="attend",
        cost_estimate=pl.CostEstimate(
            flops=flops, bytes_accessed=8 * 2**20, transcendentals=heads * span * width
        ),
    )(place, q, d, rep, outer, inner, rim_out, rim_in, *crossed_a, *crossed_b)


def finish(q, d, probs, dscores, keys_t, vals_t):
    heads, span = q.shape[:2]
    columns = probs.shape[1]
    block = span // 2

    def head(*dims):
        return pl.BlockSpec((1, *dims), lambda h: (h, 0, 0))

    return pl.pallas_call(
        finish_kernel,
        grid=(heads,),
        in_specs=[head(span, 128)] * 2 + [head(columns, span)] * 2 + [head(128, columns)] * 2,
        out_specs=[head(span, 128)] * 2 + [pl.BlockSpec((2, 1, span, 128), lambda h: (0, h, 0, 0))],
        out_shape=[
            shape((heads, span, 128)),
            shape((heads, span, 128)),
            shape((2, heads, span, 128), F32),
        ],
        scratch_shapes=[
            pltpu.VMEM((2, LEVELS, block, 128), F32),
            pltpu.VMEM((2, block, 128), F32),
        ],
        compiler_params=params(40),
        name="finish",
        cost_estimate=pl.CostEstimate(
            flops=2 * heads * span * columns * 128 * 3,
            bytes_accessed=20 * 2**20,
            transcendentals=0,
        ),
    )(q, d, probs, dscores, keys_t, vals_t)


def join_kernel(heads, place_ref, att, gq, att_out, gq_out, wide):
    span = att.shape[1]
    odd = lax.rem(place_ref[0], 2)
    for ref, out in ((att, att_out), (gq, gq_out)):
        for head in range(heads):
            wide[pl.ds(head, span, stride=heads), :] = ref[head].astype(F32)
        turned_back(out, wide, odd)


def join(place, att, gq):
    heads, span = att.shape[:2]
    return pl.pallas_call(
        functools.partial(join_kernel, heads),
        out_shape=[shape((heads * span, 128))] * 2,
        in_specs=[SMEM_SPEC, VMEM_SPEC, VMEM_SPEC],
        scratch_shapes=[pltpu.VMEM((heads * span, 128), F32)],
        compiler_params=params(12),
        name="join",
        cost_estimate=pl.CostEstimate(flops=0, bytes_accessed=4 * 2**20, transcendentals=0),
    )(place, att, gq)


def gather_kernel(heads, place_ref, own, outer, inner, *refs):
    downs, ups, outs = refs[:LEVELS], refs[LEVELS : 2 * LEVELS], refs[2 * LEVELS : 2 * LEVELS + 2]
    wide, mine, spread = refs[2 * LEVELS + 2 :]
    span = own.shape[2]
    block = span // 2
    odd = lax.rem(place_ref[0], 2)
    for which, out in enumerate(outs):
        for head in range(heads):
            both = None
            for level in reversed(range(LEVELS)):
                value = downs[level][which, head].astype(F32) + ups[level][which, head].astype(F32)
                value = value * (1.0 / 2 ** (level + 1))
                if both is not None:
                    size = both.shape[0]
                    spread[pl.ds(0, size, stride=2), :] = both
                    spread[pl.ds(1, size, stride=2), :] = both
                    value = value + spread[pl.ds(0, 2 * size), :]
                both = value
            mine[pl.ds(0, block), :] = own[which, head, :block] + outer[which, head].astype(F32)
            mine[pl.ds(block, block), :] = own[which, head, block:] + inner[which, head].astype(F32)
            for second in range(2):
                wide[pl.ds(head + heads * second, block, stride=2 * heads), :] = (
                    mine[pl.ds(second, block, stride=2), :] + both
                )
        turned_back(out, wide, odd)


def gather(place, own, *sums):
    heads, span = own.shape[1:3]
    return pl.pallas_call(
        functools.partial(gather_kernel, heads),
        out_shape=[shape((heads * span, 128))] * 2,
        in_specs=[SMEM_SPEC] + [VMEM_SPEC] * (1 + len(sums)),
        scratch_shapes=[
            pltpu.VMEM((heads * span, 128), F32),
            pltpu.VMEM((span, 128), F32),
            pltpu.VMEM((span // 2, 128), F32),
        ],
        compiler_params=params(16),
        name="gather",
        cost_estimate=pl.CostEstimate(flops=0, bytes_accessed=8 * 2**20, transcendentals=0),
    )(place, own, *sums)


def local(query, key, value, dout):
    span, heads, width = query.shape
    count = lax.axis_size("seq")
    place = jnp.reshape(lax.axis_index("seq"), (1,)).astype(jnp.int32)
    flat = (heads * span, width)
    q2, k2, v2, d2 = (x.reshape(flat) for x in (query, key, value, dout))
    outer, inner, *coarse = split_kv(place, k2, v2, heads, span)
    crossed_b, crossed_a, rims = exchange(coarse, coarse, outer, inner)
    qh, dh, rep = split_qd(place, q2, d2, heads, span)
    g_out, g_in, *grads = attend(
        place, count, qh, dh, rep, outer, inner, *rims, crossed_a, crossed_b
    )
    grads, kept = grads[: 2 * LEVELS], grads[2 * LEVELS :]
    downs, ups, rims = exchange(grads[:LEVELS], grads[LEVELS:], g_out, g_in)
    att, gq, own = finish(qh, dh, *kept)
    attended, grad_query = join(place, att, gq)
    grad_key, grad_value = gather(place, own, *rims, *downs, *ups)
    return tuple(
        x.reshape(span, heads, width) for x in (attended, grad_query, grad_key, grad_value)
    )


def solution(mesh):
    placed = P("seq", "head", None)
    return jax.shard_map(
        local,
        mesh=mesh,
        in_specs=(placed,) * 4,
        out_specs=(placed,) * 4,
        check_vma=False,
    )
```

```python
import functools
import math

import jax
import jax.numpy as jnp
from jax import lax
from jax.experimental import pallas as pl
from jax.experimental.pallas import tpu as pltpu
from jax.sharding import PartitionSpec as P

BLOCK = 256
LEVELS = 3
STEP = 32
LOG2E = math.log2(math.e)

BF = jnp.bfloat16
F32 = jnp.float32


def crossed(value, steps):
    count = lax.axis_size("seq")
    pairs = [(at, at + (steps if at % 2 == 0 else -steps)) for at in range(count)]
    return lax.ppermute(value, "seq", [(at, to) for at, to in pairs if 0 <= to < count])


def swapped(value, across):
    count = lax.axis_size("seq")
    pairs = [(at, at ^ 1) for at in range(count)]
    if across:
        pairs = [(at, at + 1 if at % 2 else at - 1) for at in range(count)]
    return lax.ppermute(value, "seq", [(at, to) for at, to in pairs if 0 <= to < count])


def nt(left, right):
    return lax.dot_general(left, right, (((1,), (1,)), ((), ())), preferred_element_type=F32)


def nn(left, right):
    return jnp.dot(left, right, preferred_element_type=F32)


def shape(dims, dtype=BF):
    return jax.ShapeDtypeStruct(dims, dtype)


def params(mib):
    return pltpu.CompilerParams(vmem_limit_bytes=mib * 2**20)


SMEM_SPEC = pl.BlockSpec(memory_space=pltpu.SMEM)
VMEM_SPEC = pl.BlockSpec(memory_space=pltpu.VMEM)


def turned(wide, ref, odd):
    half = wide.shape[0] // 2
    wide[pl.ds(pl.multiple_of(odd * half, half), half), :] = ref[:half].astype(F32)
    wide[pl.ds(pl.multiple_of((1 - odd) * half, half), half), :] = ref[half:].astype(F32)


def turned_back(ref, wide, odd):
    half = wide.shape[0] // 2
    ref[pl.ds(pl.multiple_of(odd * half, half), half), :] = wide[:half].astype(BF)
    ref[pl.ds(pl.multiple_of((1 - odd) * half, half), half), :] = wide[half:].astype(BF)


def pair_sums(wide, row, size, heads):
    return (
        wide[pl.ds(row, size, stride=2 * heads), :]
        + wide[pl.ds(row + heads, size, stride=2 * heads), :]
    )


def next_sums(sums, total):
    size = total.shape[0]
    sums[pl.ds(0, size), :] = total
    half = size // 2
    return sums[pl.ds(0, half, stride=2), :] + sums[pl.ds(1, half, stride=2), :]


def split_kv_kernel(heads, place_ref, k_ref, v_ref, outer, inner, *rest):
    coarse, (wide, sums) = rest[:LEVELS], rest[LEVELS:]
    block = inner.shape[2]
    odd = lax.rem(place_ref[0], 2)
    for at, ref in enumerate((k_ref, v_ref)):
        turned(wide, ref, odd)
        for head in range(heads):
            outer[at, head] = wide[pl.ds(head, block, stride=heads), :].astype(BF)
            inner[at, head] = wide[pl.ds(head + heads * block, block, stride=heads), :].astype(BF)
            total = pair_sums(wide, head, block, heads)
            for level in range(LEVELS):
                coarse[level][at, head] = (total * (1.0 / 2 ** (level + 1))).astype(BF)
                if level + 1 < LEVELS:
                    total = next_sums(sums, total)


def split_kv(place, k2, v2, heads, span):
    block = span // 2
    outs = [shape((2, heads, block, 128))] * 2
    outs += [shape((2, heads, span // 2 ** (level + 1), 128)) for level in range(LEVELS)]
    return pl.pallas_call(
        functools.partial(split_kv_kernel, heads),
        out_shape=outs,
        in_specs=[SMEM_SPEC, VMEM_SPEC, VMEM_SPEC],
        scratch_shapes=[
            pltpu.VMEM((heads * span, 128), F32),
            pltpu.VMEM((block, 128), F32),
        ],
        compiler_params=params(16),
        name="split_kv",
        cost_estimate=pl.CostEstimate(flops=0, bytes_accessed=4 * 2**20, transcendentals=0),
    )(place, k2, v2)


def later_kernel(count, *refs):
    for at in range(count):
        refs[len(refs) - count + at][...] = refs[at][...]


def later(after, arrays):
    return pl.pallas_call(
        functools.partial(later_kernel, len(arrays)),
        out_shape=[shape(x.shape) for x in arrays],
        in_specs=[VMEM_SPEC] * len(arrays) + [pl.BlockSpec(memory_space=pl.ANY)] * len(after),
        compiler_params=params(8),
        name="later",
        cost_estimate=pl.CostEstimate(flops=0, bytes_accessed=2 * 2**20, transcendentals=0),
    )(*arrays, *after)


def exchange(firsts, seconds, outer, inner):
    steps = [2 ** (level + 1) for level in range(LEVELS)]
    down = [crossed(x, -step) for x, step in zip(firsts, steps)]
    rims = swapped(outer, True), swapped(inner, False)
    up = [
        crossed(x, step) for x, step in zip(later((*down[1:], rims[1]), seconds), steps)
    ]
    return down, up, rims


def split_qd_kernel(heads, place_ref, q_ref, d_ref, q_out, d_out, rep_out, wide, sums, spread):
    span = q_out.shape[1]
    odd = lax.rem(place_ref[0], 2)
    turned(wide, d_ref, odd)
    for head in range(heads):
        d_out[head] = wide[pl.ds(head, span, stride=heads), :].astype(BF)
    turned(wide, q_ref, odd)
    for head in range(heads):
        q_out[head] = wide[pl.ds(head, span, stride=heads), :].astype(BF)
        total = pair_sums(wide, head, span // 2, heads)
        for level in range(LEVELS):
            factor = 2 ** (level + 1)
            mean = (total * (1.0 / factor)).astype(BF).astype(F32)
            for row in range(factor):
                spread[pl.ds(row, span // factor, stride=factor), :] = mean
            rep_out[level, head] = spread[...].astype(BF)
            if level + 1 < LEVELS:
                total = next_sums(sums, total)


def split_qd(place, q2, d2, heads, span):
    return pl.pallas_call(
        functools.partial(split_qd_kernel, heads),
        out_shape=[
            shape((heads, span, 128)),
            shape((heads, span, 128)),
            shape((LEVELS, heads, span, 128)),
        ],
        in_specs=[SMEM_SPEC] + [VMEM_SPEC] * 2,
        scratch_shapes=[
            pltpu.VMEM((heads * span, 128), F32),
            pltpu.VMEM((span // 2, 128), F32),
            pltpu.VMEM((span, 128), F32),
        ],
        compiler_params=params(16),
        name="split_qd",
        cost_estimate=pl.CostEstimate(flops=0, bytes_accessed=8 * 2**20, transcendentals=0),
    )(place, q2, d2)


def folded(x, op):
    result = x[:8]
    for row in range(8, x.shape[0], 8):
        result = op(result, x[row : row + 8])
    return result


def attend_kernel(count, place_ref, q_ref, d_ref, rep_ref, outer, inner, rim_out, rim_in, *rest):
    crossed_a, crossed_b = rest[:LEVELS], rest[LEVELS : 2 * LEVELS]
    att, gq, own, g_out, g_in = rest[2 * LEVELS : 2 * LEVELS + 5]
    rest = rest[2 * LEVELS + 5 :]
    g_as, g_bs = rest[:LEVELS], rest[LEVELS : 2 * LEVELS]
    keys, vals, keys_t, vals_t, scores, grads, probs, dscores, rows, total_q = rest[2 * LEVELS :]
    place = place_ref[0]
    even = lax.rem(place, 2) == 0
    block = outer.shape[2]
    scale = 1.0 / math.sqrt(128)
    scale2 = scale * LOG2E

    def reaches(below, steps):
        return jnp.where(below, place >= steps, place < count - steps)

    parts = [(rim_out, reaches(even, 1), 0), (outer, None, 0), (inner, None, 0)]
    for level in range(LEVELS):
        factor = 2 ** (level + 1)
        parts.append((crossed_a[level], reaches(even, factor), level + 1))
        parts.append((crossed_b[level], reaches(jnp.logical_not(even), factor), level + 1))
    parts.append((rim_in, None, 0))
    at = 0
    segments = []
    for ref, ok, level in parts:
        size = ref.shape[2]
        keys[pl.ds(at, size), :] = ref[0, 0]
        vals[pl.ds(at, size), :] = ref[1, 0]
        bias = float(level)
        if ok is not None:
            bias = jnp.where(ok, bias, -jnp.inf).astype(F32)
        segments.append((at, size, bias, level))
        at += size
    columns = at
    keys_t[...] = keys[...].T
    vals_t[...] = vals[...].T

    turns = (0, 1)
    cols = [pl.ds(turn * block, block) for turn in turns]
    met = [segments[:-1], segments[1:]]
    top = [None, None]
    for turn in turns:
        d_blk = d_ref[0, cols[turn], :]
        using = [q_ref[0, cols[turn], :]]
        using += [rep_ref[level, 0, cols[turn], :] for level in range(LEVELS)]
        for start, size, bias, level in met[turn]:
            here = pl.ds(start, size)
            s = nt(keys[here, :], using[level])
            scores[turn, here, :] = s
            high = jnp.max(folded(s, jnp.maximum), axis=0, keepdims=True) * scale2 + bias
            top[turn] = high if top[turn] is None else jnp.maximum(top[turn], high)
            grads[turn, here, :] = nt(vals[here, :], d_blk)
    inverse, delta = [None, None], [None, None]
    for turn in turns:
        total = jnp.zeros((8, block), F32)
        acc = jnp.zeros((8, block), F32)
        for start, size, bias, level in met[turn]:
            shift = top[turn] - bias
            for row in range(start, start + size, STEP):
                here = pl.ds(row, STEP)
                e = jnp.exp2(scores[turn, here, :] * scale2 - shift)
                scores[turn, here, :] = e
                total = total + folded(e, jnp.add)
                acc = acc + folded(e * grads[turn, here, :], jnp.add)
        inverse[turn] = 1.0 / jnp.sum(total, axis=0, keepdims=True)
        delta[turn] = jnp.sum(acc, axis=0, keepdims=True) * inverse[turn]
    for turn in turns:
        for row in range(met[turn][0][0], met[turn][-1][0] + met[turn][-1][1], STEP):
            here = pl.ds(row, STEP)
            p = scores[turn, here, :] * inverse[turn]
            probs[here, cols[turn]] = p.astype(BF)
            dscores[here, cols[turn]] = (p * (grads[turn, here, :] - delta[turn])).astype(BF)
        first, last = met[turn][0][0], met[turn][-1][0] + met[turn][-1][1]
        up = nn(vals_t[:, first:last], probs[first:last, cols[turn]])
        att[0, cols[turn], :] = up.T.astype(BF)
        if turn == 0:
            fine = nn(keys_t[:, : 3 * block], dscores[: 3 * block, cols[turn]])
        else:
            fine = nn(keys_t[:, block : 3 * block], dscores[block : 3 * block, cols[turn]])
            tail = columns - block
            fine = fine + nn(keys_t[:, tail:], dscores[tail:, cols[turn]])
        total_q[turn] = fine.T
        for level in range(1, LEVELS + 1):
            spots = [(s, z) for s, z, _, lev in segments if lev == level]
            start, size = spots[0][0], spots[0][1] + spots[1][1]
            up = nn(keys_t[:, start : start + size], dscores[start : start + size, cols[turn]])
            rows[turn, level - 1] = up.T
            factor = 2**level
            groups = block // factor
            mean = rows[turn, level - 1, pl.ds(0, groups, stride=factor), :]
            for row in range(1, factor):
                mean = mean + rows[turn, level - 1, pl.ds(row, groups, stride=factor), :]
            mean = mean * (1.0 / factor)
            for row in range(factor):
                spot = pl.ds(row, groups, stride=factor)
                total_q[turn, spot, :] = total_q[turn, spot, :] + mean
        gq[0, cols[turn], :] = (total_q[turn] * scale).astype(BF)

    places = [(g_out, None), (own, 0), (own, block)]
    for level in range(LEVELS):
        places += [(g_as[level], None), (g_bs[level], None)]
    places.append((g_in, None))
    for (ref, offset), (start, size, bias, level) in zip(places, segments):
        queries = pl.ds(0, 2 * block)
        if ref is g_out:
            queries = cols[0]
        if ref is g_in:
            queries = cols[1]
        right = rep_ref[level - 1, 0, queries, :] if level else q_ref[0, queries, :]
        here = pl.ds(start, size)
        gk = nn(dscores[here, queries], right) * scale
        gv = nn(probs[here, queries], d_ref[0, queries, :])
        for which, value in enumerate((gk, gv)):
            if offset is None:
                ref[which, 0] = value.astype(BF)
            else:
                ref[which, 0, pl.ds(offset, size), :] = value


def attend(place, count, q, d, rep, outer, inner, rim_out, rim_in, crossed_a, crossed_b):
    heads, block = inner.shape[1], inner.shape[2]
    span = 2 * block
    sizes = [span // 2 ** (level + 1) for level in range(LEVELS)]
    columns = 4 * block + 2 * sum(sizes)
    width = columns - block

    def pair(size):
        return pl.BlockSpec((2, 1, size, 128), lambda h: (0, h, 0, 0))

    head_spec = pl.BlockSpec((1, span, 128), lambda h: (h, 0, 0))
    flops = 2 * heads * span * width * 128 * 6
    return pl.pallas_call(
        functools.partial(attend_kernel, count),
        grid=(heads,),
        in_specs=[
            SMEM_SPEC,
            head_spec,
            head_spec,
            pl.BlockSpec((LEVELS, 1, span, 128), lambda h: (0, h, 0, 0)),
        ]
        + [pair(block)] * 4
        + [pair(size) for size in sizes] * 2,
        out_specs=[head_spec, head_spec, pair(span), pair(block), pair(block)]
        + [pair(size) for size in sizes] * 2,
        out_shape=[
            shape((heads, span, 128)),
            shape((heads, span, 128)),
            shape((2, heads, span, 128), F32),
            shape((2, heads, block, 128)),
            shape((2, heads, block, 128)),
        ]
        + [shape((2, heads, size, 128)) for size in sizes] * 2,
        scratch_shapes=[
            pltpu.VMEM((columns, 128), BF),
            pltpu.VMEM((columns, 128), BF),
            pltpu.VMEM((128, columns), BF),
            pltpu.VMEM((128, columns), BF),
            pltpu.VMEM((2, columns, block), F32),
            pltpu.VMEM((2, columns, block), F32),
            pltpu.VMEM((columns, span), BF),
            pltpu.VMEM((columns, span), BF),
            pltpu.VMEM((2, LEVELS, block, 128), F32),
            pltpu.VMEM((2, block, 128), F32),
        ],
        compiler_params=params(30),
        name="attend",
        cost_estimate=pl.CostEstimate(
            flops=flops, bytes_accessed=8 * 2**20, transcendentals=heads * span * width
        ),
    )(place, q, d, rep, outer, inner, rim_out, rim_in, *crossed_a, *crossed_b)


def join_kernel(heads, place_ref, att, gq, att_out, gq_out, wide):
    span = att.shape[1]
    odd = lax.rem(place_ref[0], 2)
    for ref, out in ((att, att_out), (gq, gq_out)):
        for head in range(heads):
            wide[pl.ds(head, span, stride=heads), :] = ref[head].astype(F32)
        turned_back(out, wide, odd)


def join(place, att, gq):
    heads, span = att.shape[:2]
    return pl.pallas_call(
        functools.partial(join_kernel, heads),
        out_shape=[shape((heads * span, 128))] * 2,
        in_specs=[SMEM_SPEC, VMEM_SPEC, VMEM_SPEC],
        scratch_shapes=[pltpu.VMEM((heads * span, 128), F32)],
        compiler_params=params(12),
        name="join",
        cost_estimate=pl.CostEstimate(flops=0, bytes_accessed=4 * 2**20, transcendentals=0),
    )(place, att, gq)


def gather_kernel(heads, place_ref, own, outer, inner, *refs):
    downs, ups, outs = refs[:LEVELS], refs[LEVELS : 2 * LEVELS], refs[2 * LEVELS : 2 * LEVELS + 2]
    wide, mine, spread = refs[2 * LEVELS + 2 :]
    span = own.shape[2]
    block = span // 2
    odd = lax.rem(place_ref[0], 2)
    for which, out in enumerate(outs):
        for head in range(heads):
            both = None
            for level in reversed(range(LEVELS)):
                value = downs[level][which, head].astype(F32) + ups[level][which, head].astype(F32)
                value = value * (1.0 / 2 ** (level + 1))
                if both is not None:
                    size = both.shape[0]
                    spread[pl.ds(0, size, stride=2), :] = both
                    spread[pl.ds(1, size, stride=2), :] = both
                    value = value + spread[pl.ds(0, 2 * size), :]
                both = value
            mine[pl.ds(0, block), :] = own[which, head, :block] + outer[which, head].astype(F32)
            mine[pl.ds(block, block), :] = own[which, head, block:] + inner[which, head].astype(F32)
            for second in range(2):
                wide[pl.ds(head + heads * second, block, stride=2 * heads), :] = (
                    mine[pl.ds(second, block, stride=2), :] + both
                )
        turned_back(out, wide, odd)


def gather(place, own, *sums):
    heads, span = own.shape[1:3]
    return pl.pallas_call(
        functools.partial(gather_kernel, heads),
        out_shape=[shape((heads * span, 128))] * 2,
        in_specs=[SMEM_SPEC] + [VMEM_SPEC] * (1 + len(sums)),
        scratch_shapes=[
            pltpu.VMEM((heads * span, 128), F32),
            pltpu.VMEM((span, 128), F32),
            pltpu.VMEM((span // 2, 128), F32),
        ],
        compiler_params=params(16),
        name="gather",
        cost_estimate=pl.CostEstimate(flops=0, bytes_accessed=8 * 2**20, transcendentals=0),
    )(place, own, *sums)


def local(query, key, value, dout):
    span, heads, width = query.shape
    count = lax.axis_size("seq")
    place = jnp.reshape(lax.axis_index("seq"), (1,)).astype(jnp.int32)
    flat = (heads * span, width)
    q2, k2, v2, d2 = (x.reshape(flat) for x in (query, key, value, dout))
    outer, inner, *coarse = split_kv(place, k2, v2, heads, span)
    crossed_b, crossed_a, rims = exchange(coarse, coarse, outer, inner)
    qh, dh, rep = split_qd(place, q2, d2, heads, span)
    att, gq, own, g_out, g_in, *grads = attend(
        place, count, qh, dh, rep, outer, inner, *rims, crossed_a, crossed_b
    )
    downs, ups, rims = exchange(grads[:LEVELS], grads[LEVELS:], g_out, g_in)
    attended, grad_query = join(place, att, gq)
    grad_key, grad_value = gather(place, own, *rims, *downs, *ups)
    return tuple(
        x.reshape(span, heads, width) for x in (attended, grad_query, grad_key, grad_value)
    )


def solution(mesh):
    placed = P("seq", "head", None)
    return jax.shard_map(
        local,
        mesh=mesh,
        in_specs=(placed,) * 4,
        out_specs=(placed,) * 4,
        check_vma=False,
    )
```

```python
import functools
import math

import jax
import jax.numpy as jnp
from jax import lax
from jax.experimental import pallas as pl
from jax.experimental.pallas import tpu as pltpu
from jax.sharding import PartitionSpec as P

BLOCK = 256
LEVELS = 3
STEP = 32
LOG2E = math.log2(math.e)

BF = jnp.bfloat16
F32 = jnp.float32


def crossed(value, steps):
    count = lax.axis_size("seq")
    pairs = [(at, at + (steps if at % 2 == 0 else -steps)) for at in range(count)]
    return lax.ppermute(value, "seq", [(at, to) for at, to in pairs if 0 <= to < count])


def swapped(value, across):
    count = lax.axis_size("seq")
    pairs = [(at, at ^ 1) for at in range(count)]
    if across:
        pairs = [(at, at + 1 if at % 2 else at - 1) for at in range(count)]
    return lax.ppermute(value, "seq", [(at, to) for at, to in pairs if 0 <= to < count])


def nn(left, right):
    return jnp.dot(left, right, preferred_element_type=F32)


def shape(dims, dtype=BF):
    return jax.ShapeDtypeStruct(dims, dtype)


def params(mib):
    return pltpu.CompilerParams(vmem_limit_bytes=mib * 2**20)


SMEM_SPEC = pl.BlockSpec(memory_space=pltpu.SMEM)
VMEM_SPEC = pl.BlockSpec(memory_space=pltpu.VMEM)


def turned(wide, ref, odd):
    half = wide.shape[0] // 2
    wide[pl.ds(pl.multiple_of(odd * half, half), half), :] = ref[:half].astype(F32)
    wide[pl.ds(pl.multiple_of((1 - odd) * half, half), half), :] = ref[half:].astype(F32)


def turned_back(ref, wide, odd):
    half = wide.shape[0] // 2
    ref[pl.ds(pl.multiple_of(odd * half, half), half), :] = wide[:half].astype(BF)
    ref[pl.ds(pl.multiple_of((1 - odd) * half, half), half), :] = wide[half:].astype(BF)


def pair_sums(wide, row, size, heads):
    return (
        wide[pl.ds(row, size, stride=2 * heads), :]
        + wide[pl.ds(row + heads, size, stride=2 * heads), :]
    )


def next_sums(sums, total):
    size = total.shape[0]
    sums[pl.ds(0, size), :] = total
    half = size // 2
    return sums[pl.ds(0, half, stride=2), :] + sums[pl.ds(1, half, stride=2), :]


def split_kv_kernel(heads, place_ref, k_ref, v_ref, outer, inner, *rest):
    coarse, (wide, sums) = rest[:LEVELS], rest[LEVELS:]
    block = inner.shape[2]
    odd = lax.rem(place_ref[0], 2)
    for at, ref in enumerate((k_ref, v_ref)):
        turned(wide, ref, odd)
        for head in range(heads):
            outer[at, head] = wide[pl.ds(head, block, stride=heads), :].astype(BF)
            inner[at, head] = wide[pl.ds(head + heads * block, block, stride=heads), :].astype(BF)
            total = pair_sums(wide, head, block, heads)
            for level in range(LEVELS):
                coarse[level][at, head] = (total * (1.0 / 2 ** (level + 1))).astype(BF)
                if level + 1 < LEVELS:
                    total = next_sums(sums, total)


def split_kv(place, k2, v2, heads, span):
    block = span // 2
    outs = [shape((2, heads, block, 128))] * 2
    outs += [shape((2, heads, span // 2 ** (level + 1), 128)) for level in range(LEVELS)]
    return pl.pallas_call(
        functools.partial(split_kv_kernel, heads),
        out_shape=outs,
        in_specs=[SMEM_SPEC, VMEM_SPEC, VMEM_SPEC],
        scratch_shapes=[
            pltpu.VMEM((heads * span, 128), F32),
            pltpu.VMEM((block, 128), F32),
        ],
        compiler_params=params(16),
        name="split_kv",
        cost_estimate=pl.CostEstimate(flops=0, bytes_accessed=4 * 2**20, transcendentals=0),
    )(place, k2, v2)


def later_kernel(count, *refs):
    for at in range(count):
        refs[len(refs) - count + at][...] = refs[at][...]


def later(after, arrays):
    return pl.pallas_call(
        functools.partial(later_kernel, len(arrays)),
        out_shape=[shape(x.shape) for x in arrays],
        in_specs=[VMEM_SPEC] * len(arrays) + [pl.BlockSpec(memory_space=pl.ANY)] * len(after),
        compiler_params=params(8),
        name="later",
        cost_estimate=pl.CostEstimate(flops=0, bytes_accessed=2 * 2**20, transcendentals=0),
    )(*arrays, *after)


def exchange(firsts, seconds, outer, inner):
    steps = [2 ** (level + 1) for level in range(LEVELS)]
    down = [crossed(x, -step) for x, step in zip(firsts, steps)]
    rims = swapped(outer, True), swapped(inner, False)
    up = [
        crossed(x, step) for x, step in zip(later((*down[1:], rims[1]), seconds), steps)
    ]
    return down, up, rims


def split_qd_kernel(heads, place_ref, q_ref, d_ref, *refs):
    q_out, d_out, rep_out, q_turn, d_turn, rep_turn, wide, sums, spread = refs
    span = q_out.shape[1]
    odd = lax.rem(place_ref[0], 2)
    turned(wide, d_ref, odd)
    for head in range(heads):
        d_out[head] = wide[pl.ds(head, span, stride=heads), :].astype(BF)
        d_turn[head] = d_out[head].T
    turned(wide, q_ref, odd)
    for head in range(heads):
        q_out[head] = wide[pl.ds(head, span, stride=heads), :].astype(BF)
        q_turn[head] = q_out[head].T
        total = pair_sums(wide, head, span // 2, heads)
        for level in range(LEVELS):
            factor = 2 ** (level + 1)
            mean = (total * (1.0 / factor)).astype(BF).astype(F32)
            for row in range(factor):
                spread[pl.ds(row, span // factor, stride=factor), :] = mean
            rep_out[level, head] = spread[...].astype(BF)
            rep_turn[level, head] = rep_out[level, head].T
            if level + 1 < LEVELS:
                total = next_sums(sums, total)


def split_qd(place, q2, d2, heads, span):
    return pl.pallas_call(
        functools.partial(split_qd_kernel, heads),
        out_shape=[
            shape((heads, span, 128)),
            shape((heads, span, 128)),
            shape((LEVELS, heads, span, 128)),
            shape((heads, 128, span)),
            shape((heads, 128, span)),
            shape((LEVELS, heads, 128, span)),
        ],
        in_specs=[SMEM_SPEC] + [VMEM_SPEC] * 2,
        scratch_shapes=[
            pltpu.VMEM((heads * span, 128), F32),
            pltpu.VMEM((span // 2, 128), F32),
            pltpu.VMEM((span, 128), F32),
        ],
        compiler_params=params(16),
        name="split_qd",
        cost_estimate=pl.CostEstimate(flops=0, bytes_accessed=8 * 2**20, transcendentals=0),
    )(place, q2, d2)


def folded(x, op):
    result = x[:8]
    for row in range(8, x.shape[0], 8):
        result = op(result, x[row : row + 8])
    return result


def attend_kernel(
    count, place_ref, q_ref, d_ref, rep_ref, q_turn, d_turn, rep_turn, outer, inner, *rest
):
    rim_out, rim_in, *rest = rest
    crossed_a, crossed_b = rest[:LEVELS], rest[LEVELS : 2 * LEVELS]
    att, gq, own, g_out, g_in = rest[2 * LEVELS : 2 * LEVELS + 5]
    rest = rest[2 * LEVELS + 5 :]
    g_as, g_bs = rest[:LEVELS], rest[LEVELS : 2 * LEVELS]
    keys, vals, keys_t, vals_t, scores, grads, probs, dscores, rows, total_q = rest[2 * LEVELS :]
    place = place_ref[0]
    even = lax.rem(place, 2) == 0
    block = outer.shape[2]
    scale = 1.0 / math.sqrt(128)
    scale2 = scale * LOG2E

    def reaches(below, steps):
        return jnp.where(below, place >= steps, place < count - steps)

    parts = [(rim_out, reaches(even, 1), 0), (outer, None, 0), (inner, None, 0)]
    for level in range(LEVELS):
        factor = 2 ** (level + 1)
        parts.append((crossed_a[level], reaches(even, factor), level + 1))
        parts.append((crossed_b[level], reaches(jnp.logical_not(even), factor), level + 1))
    parts.append((rim_in, None, 0))
    at = 0
    segments = []
    for ref, ok, level in parts:
        size = ref.shape[2]
        keys[pl.ds(at, size), :] = ref[0, 0]
        vals[pl.ds(at, size), :] = ref[1, 0]
        bias = float(level)
        if ok is not None:
            bias = jnp.where(ok, bias, -jnp.inf).astype(F32)
        segments.append((at, size, bias, level))
        at += size
    columns = at
    keys_t[...] = keys[...].T
    vals_t[...] = vals[...].T

    turns = (0, 1)
    cols = [pl.ds(turn * block, block) for turn in turns]
    met = [segments[:-1], segments[1:]]
    top = [None, None]
    for turn in turns:
        d_blk = d_turn[0, :, cols[turn]]
        using = [q_turn[0, :, cols[turn]]]
        using += [rep_turn[level, 0, :, cols[turn]] for level in range(LEVELS)]
        for start, size, bias, level in met[turn]:
            here = pl.ds(start, size)
            s = nn(keys[here, :], using[level])
            scores[turn, here, :] = s
            high = jnp.max(folded(s, jnp.maximum), axis=0, keepdims=True) * scale2 + bias
            top[turn] = high if top[turn] is None else jnp.maximum(top[turn], high)
            grads[turn, here, :] = nn(vals[here, :], d_blk)
    inverse, delta = [None, None], [None, None]
    for turn in turns:
        total = jnp.zeros((8, block), F32)
        acc = jnp.zeros((8, block), F32)
        for start, size, bias, level in met[turn]:
            shift = top[turn] - bias
            for row in range(start, start + size, STEP):
                here = pl.ds(row, STEP)
                e = jnp.exp2(scores[turn, here, :] * scale2 - shift)
                scores[turn, here, :] = e
                total = total + folded(e, jnp.add)
                acc = acc + folded(e * grads[turn, here, :], jnp.add)
        inverse[turn] = 1.0 / jnp.sum(total, axis=0, keepdims=True)
        delta[turn] = jnp.sum(acc, axis=0, keepdims=True) * inverse[turn]
    for turn in turns:
        for row in range(met[turn][0][0], met[turn][-1][0] + met[turn][-1][1], STEP):
            here = pl.ds(row, STEP)
            p = scores[turn, here, :] * inverse[turn]
            probs[here, cols[turn]] = p.astype(BF)
            dscores[here, cols[turn]] = (p * (grads[turn, here, :] - delta[turn])).astype(BF)
        first, last = met[turn][0][0], met[turn][-1][0] + met[turn][-1][1]
        up = nn(vals_t[:, first:last], probs[first:last, cols[turn]])
        att[0, cols[turn], :] = up.T.astype(BF)
        if turn == 0:
            fine = nn(keys_t[:, : 3 * block], dscores[: 3 * block, cols[turn]])
        else:
            fine = nn(keys_t[:, block : 3 * block], dscores[block : 3 * block, cols[turn]])
            tail = columns - block
            fine = fine + nn(keys_t[:, tail:], dscores[tail:, cols[turn]])
        total_q[turn] = fine.T
        for level in range(1, LEVELS + 1):
            spots = [(s, z) for s, z, _, lev in segments if lev == level]
            start, size = spots[0][0], spots[0][1] + spots[1][1]
            up = nn(keys_t[:, start : start + size], dscores[start : start + size, cols[turn]])
            rows[turn, level - 1] = up.T
            factor = 2**level
            groups = block // factor
            mean = rows[turn, level - 1, pl.ds(0, groups, stride=factor), :]
            for row in range(1, factor):
                mean = mean + rows[turn, level - 1, pl.ds(row, groups, stride=factor), :]
            mean = mean * (1.0 / factor)
            for row in range(factor):
                spot = pl.ds(row, groups, stride=factor)
                total_q[turn, spot, :] = total_q[turn, spot, :] + mean
        gq[0, cols[turn], :] = (total_q[turn] * scale).astype(BF)

    places = [(g_out, None), (own, 0), (own, block)]
    for level in range(LEVELS):
        places += [(g_as[level], None), (g_bs[level], None)]
    places.append((g_in, None))
    for (ref, offset), (start, size, bias, level) in zip(places, segments):
        queries = pl.ds(0, 2 * block)
        if ref is g_out:
            queries = cols[0]
        if ref is g_in:
            queries = cols[1]
        right = rep_ref[level - 1, 0, queries, :] if level else q_ref[0, queries, :]
        here = pl.ds(start, size)
        gk = nn(dscores[here, queries], right) * scale
        gv = nn(probs[here, queries], d_ref[0, queries, :])
        for which, value in enumerate((gk, gv)):
            if offset is None:
                ref[which, 0] = value.astype(BF)
            else:
                ref[which, 0, pl.ds(offset, size), :] = value


def attend(place, count, q, d, rep, turned_qd, outer, inner, rim_out, rim_in, crossed_a, crossed_b):
    heads, block = inner.shape[1], inner.shape[2]
    span = 2 * block
    sizes = [span // 2 ** (level + 1) for level in range(LEVELS)]
    columns = 4 * block + 2 * sum(sizes)
    width = columns - block

    def pair(size):
        return pl.BlockSpec((2, 1, size, 128), lambda h: (0, h, 0, 0))

    head_spec = pl.BlockSpec((1, span, 128), lambda h: (h, 0, 0))
    flops = 2 * heads * span * width * 128 * 6
    return pl.pallas_call(
        functools.partial(attend_kernel, count),
        grid=(heads,),
        in_specs=[
            SMEM_SPEC,
            head_spec,
            head_spec,
            pl.BlockSpec((LEVELS, 1, span, 128), lambda h: (0, h, 0, 0)),
            pl.BlockSpec((1, 128, span), lambda h: (h, 0, 0)),
            pl.BlockSpec((1, 128, span), lambda h: (h, 0, 0)),
            pl.BlockSpec((LEVELS, 1, 128, span), lambda h: (0, h, 0, 0)),
        ]
        + [pair(block)] * 4
        + [pair(size) for size in sizes] * 2,
        out_specs=[head_spec, head_spec, pair(span), pair(block), pair(block)]
        + [pair(size) for size in sizes] * 2,
        out_shape=[
            shape((heads, span, 128)),
            shape((heads, span, 128)),
            shape((2, heads, span, 128), F32),
            shape((2, heads, block, 128)),
            shape((2, heads, block, 128)),
        ]
        + [shape((2, heads, size, 128)) for size in sizes] * 2,
        scratch_shapes=[
            pltpu.VMEM((columns, 128), BF),
            pltpu.VMEM((columns, 128), BF),
            pltpu.VMEM((128, columns), BF),
            pltpu.VMEM((128, columns), BF),
            pltpu.VMEM((2, columns, block), F32),
            pltpu.VMEM((2, columns, block), F32),
            pltpu.VMEM((columns, span), BF),
            pltpu.VMEM((columns, span), BF),
            pltpu.VMEM((2, LEVELS, block, 128), F32),
            pltpu.VMEM((2, block, 128), F32),
        ],
        compiler_params=params(30),
        name="attend",
        cost_estimate=pl.CostEstimate(
            flops=flops, bytes_accessed=8 * 2**20, transcendentals=heads * span * width
        ),
    )(place, q, d, rep, *turned_qd, outer, inner, rim_out, rim_in, *crossed_a, *crossed_b)


def join_kernel(heads, place_ref, att, gq, att_out, gq_out, wide):
    span = att.shape[1]
    odd = lax.rem(place_ref[0], 2)
    for ref, out in ((att, att_out), (gq, gq_out)):
        for head in range(heads):
            wide[pl.ds(head, span, stride=heads), :] = ref[head].astype(F32)
        turned_back(out, wide, odd)


def join(place, att, gq):
    heads, span = att.shape[:2]
    return pl.pallas_call(
        functools.partial(join_kernel, heads),
        out_shape=[shape((heads * span, 128))] * 2,
        in_specs=[SMEM_SPEC, VMEM_SPEC, VMEM_SPEC],
        scratch_shapes=[pltpu.VMEM((heads * span, 128), F32)],
        compiler_params=params(12),
        name="join",
        cost_estimate=pl.CostEstimate(flops=0, bytes_accessed=4 * 2**20, transcendentals=0),
    )(place, att, gq)


def gather_kernel(heads, place_ref, own, outer, inner, *refs):
    downs, ups, outs = refs[:LEVELS], refs[LEVELS : 2 * LEVELS], refs[2 * LEVELS : 2 * LEVELS + 2]
    wide, mine, spread = refs[2 * LEVELS + 2 :]
    span = own.shape[2]
    block = span // 2
    odd = lax.rem(place_ref[0], 2)
    for which, out in enumerate(outs):
        for head in range(heads):
            both = None
            for level in reversed(range(LEVELS)):
                value = downs[level][which, head].astype(F32) + ups[level][which, head].astype(F32)
                value = value * (1.0 / 2 ** (level + 1))
                if both is not None:
                    size = both.shape[0]
                    spread[pl.ds(0, size, stride=2), :] = both
                    spread[pl.ds(1, size, stride=2), :] = both
                    value = value + spread[pl.ds(0, 2 * size), :]
                both = value
            mine[pl.ds(0, block), :] = own[which, head, :block] + outer[which, head].astype(F32)
            mine[pl.ds(block, block), :] = own[which, head, block:] + inner[which, head].astype(F32)
            for second in range(2):
                wide[pl.ds(head + heads * second, block, stride=2 * heads), :] = (
                    mine[pl.ds(second, block, stride=2), :] + both
                )
        turned_back(out, wide, odd)


def gather(place, own, *sums):
    heads, span = own.shape[1:3]
    return pl.pallas_call(
        functools.partial(gather_kernel, heads),
        out_shape=[shape((heads * span, 128))] * 2,
        in_specs=[SMEM_SPEC] + [VMEM_SPEC] * (1 + len(sums)),
        scratch_shapes=[
            pltpu.VMEM((heads * span, 128), F32),
            pltpu.VMEM((span, 128), F32),
            pltpu.VMEM((span // 2, 128), F32),
        ],
        compiler_params=params(16),
        name="gather",
        cost_estimate=pl.CostEstimate(flops=0, bytes_accessed=8 * 2**20, transcendentals=0),
    )(place, own, *sums)


def local(query, key, value, dout):
    span, heads, width = query.shape
    count = lax.axis_size("seq")
    place = jnp.reshape(lax.axis_index("seq"), (1,)).astype(jnp.int32)
    flat = (heads * span, width)
    q2, k2, v2, d2 = (x.reshape(flat) for x in (query, key, value, dout))
    outer, inner, *coarse = split_kv(place, k2, v2, heads, span)
    crossed_b, crossed_a, rims = exchange(coarse, coarse, outer, inner)
    qh, dh, rep, *turned_qd = split_qd(place, q2, d2, heads, span)
    att, gq, own, g_out, g_in, *grads = attend(
        place, count, qh, dh, rep, turned_qd, outer, inner, *rims, crossed_a, crossed_b
    )
    downs, ups, rims = exchange(grads[:LEVELS], grads[LEVELS:], g_out, g_in)
    attended, grad_query = join(place, att, gq)
    grad_key, grad_value = gather(place, own, *rims, *downs, *ups)
    return tuple(
        x.reshape(span, heads, width) for x in (attended, grad_query, grad_key, grad_value)
    )


def solution(mesh):
    placed = P("seq", "head", None)
    return jax.shard_map(
        local,
        mesh=mesh,
        in_specs=(placed,) * 4,
        out_specs=(placed,) * 4,
        check_vma=False,
    )
```
